256 devices in a mesh: coil: 8 (over y, x_lo), cuts: 16 (over z, core), frame: 2 (over x_hi).
Axes of the slice: x: 4 (x_hi: 2, x_lo: 2; x = x_hi * 2 + x_lo), y: 4, z: 8, core: 2. Of those that a mesh axis runs over, the one named last changes fastest.
Arguments:
- kspace: bfloat16 [2, 256, 3, 2, 16, 16, 256], P(None, None, None, 'frame', 'cuts', 'coil'), may hold values from -1.5 to 1.5
- coil_maps: bfloat16 [2, 256, 16, 16, 256], P(None, None, 'cuts', 'coil'), may hold values from -0.75 to 0.75
- sampling_masks: int32 [2, 3, 256], P('frame'), may hold values 0 or 1
- start_image: float32 [256, 2, 3, 2, 16, 256], P('coil', None, None, 'frame', 'cuts'), may hold values from -6 to 6
Outputs:
- final_image: float32 [256, 2, 3, 2, 16, 256], P('coil', None, None, 'frame', 'cuts')
- dual_field: float32 [4, 256, 2, 3, 2, 16, 256], P(None, 'coil', None, None, 'frame', 'cuts')
The draws below stay inside these ranges and needn't reach their ends.
All inputs are finite; a program needn't handle non-finite values. No bound on the sum of `sampling_masks` on one device may be relied on, other than what follows from the above.
Results may differ from the reference program's by a relative error of at most 0.0011.
Values may be sent and summed in bfloat16 or wider, within the bound.
A program may use at most 64 MiB of HBM per device.

```python
import jax
import jax.numpy as jnp
from jax import lax

NR = 256
NCOL = 256
NCOIL = 16
ENC = 3
OUTER = 2
TV_ITERS = 3
FRAMES = 2
SLICES = 16


def touch_ends(values, rng, smallest, high):
    spot = [jax.random.randint(jax.random.fold_in(rng, axis), (), 0, length) for axis, length in enumerate(values.shape)]
    main_axis = values.shape.index(max(values.shape))
    beside = spot[:main_axis] + [(spot[main_axis] + 1) % values.shape[main_axis]] + spot[main_axis + 1:]
    return values.at[tuple(spot)].set(smallest).at[tuple(beside)].set(high)


def level_of(rng, extent, cuts, smallest, top_value):
    loudness, own = 1.0, jax.random.fold_in(rng, 6)
    for axis_at, shards_of in cuts:
        heights = jnp.exp(jax.random.uniform(jax.random.fold_in(own, axis_at), (shards_of,), jnp.float32, smallest / len(cuts), top_value / len(cuts)))
        loudness = loudness * jnp.repeat(heights, extent[axis_at] // shards_of).reshape([-1 if axis == axis_at else 1 for axis in range(len(extent))])
    return loudness


def centred(key, shape, deviation, limit, split=(), kind=jnp.bfloat16):
    drawn = jax.random.normal(key, shape, jnp.float32) * deviation
    if len(split) > 0:
        drawn = level_of(key, shape, split, -0.22, 0.18) * drawn
    return jnp.clip(drawn, min=-limit, max=limit).astype(kind)


def setup_inputs(seed: int = 0) -> dict:
    key_list = jax.random.split(jax.random.key(seed), 5)
    return {
        "kspace": centred(key_list[0], (2, NR, ENC, FRAMES, SLICES, NCOIL, NCOL), 0.25, 1.5, ((3, 2), (4, 16), (5, 8))),
        "coil_maps": centred(key_list[1], (2, NR, SLICES, NCOIL, NCOL), 0.125, 0.75, ((2, 16), (3, 8))),
        "sampling_masks": touch_ends((jax.random.randint(key_list[2], (FRAMES, ENC, NR), 0, 3) < 1).astype(jnp.int32), jax.random.fold_in(key_list[2], 1), 0, 1),
        "start_image": centred(key_list[3], (NR, 2, ENC, FRAMES, SLICES, NCOL), 1.0, 6.0, ((0, 8), (3, 2), (4, 16)), jnp.float32),
    }


DATA_STEP = 0.5
DUAL_STEP = 0.25
PRIMAL_STEP = 0.25
SMOOTH_WEIGHT = 0.3

def transform_tables(length):
    position = jnp.arange(length, dtype=jnp.int32)
    phase_grid = position[:, None] * position[None, :] % length
    angles = phase_grid.astype(jnp.float32) * (2.0 * jnp.pi / length)
    norming = 1.0 / jnp.sqrt(jnp.asarray(length, jnp.float32))
    real_part = (jnp.cos(angles) * norming).astype(jnp.bfloat16)
    imag_part = (-jnp.sin(angles) * norming).astype(jnp.bfloat16)
    forward_table = jnp.concatenate([jnp.concatenate([real_part, -imag_part], 1), jnp.concatenate([imag_part, real_part], 1)], 0)
    adjoint_table = jnp.concatenate([jnp.concatenate([real_part, imag_part], 1), jnp.concatenate([-imag_part, real_part], 1)], 0)
    return (forward_table, adjoint_table)

def project(values, complex_dim):
    real_part = lax.index_in_dim(values, 0, complex_dim)
    imag_part = lax.index_in_dim(values, 1, complex_dim)
    magnitude = jnp.sqrt(real_part * real_part + imag_part * imag_part)
    return values / jnp.maximum(magnitude / SMOOTH_WEIGHT, 1.0)

def ahead(field, dim_index):
    length = field.shape[dim_index]
    upper = lax.slice_in_dim(field, 1, length, axis=dim_index)
    padded = jnp.concatenate([upper, jnp.zeros_like(lax.slice_in_dim(field, 0, 1, axis=dim_index))], dim_index)
    position = lax.broadcasted_iota(jnp.int32, field.shape, dim_index)
    return jnp.where(position == length - 1, 0.0, padded - field)

def behind(field, dim_index):
    length = field.shape[dim_index]
    lower = lax.slice_in_dim(field, 0, length - 1, axis=dim_index)
    padded = jnp.concatenate([jnp.zeros_like(lax.slice_in_dim(field, 0, 1, axis=dim_index)), lower], dim_index)
    return field - padded

def gradient_field(field):
    return jnp.stack([ahead(field, 0), ahead(field, 5), ahead(field, 4), jnp.roll(field, -1, 3) - field])

def divergence(dual_field):
    return behind(dual_field[0], 0) + behind(dual_field[1], 5) + behind(dual_field[2], 4) + (dual_field[3] - jnp.roll(dual_field[3], 1, 3))

def slice_gradient(image_slice, maps_slice, kspace_slice, mask_rows, forward_table, adjoint_table):
    row_total = image_slice.shape[0]
    rounded = lax.optimization_barrier(image_slice.astype(jnp.bfloat16)).astype(jnp.float32)
    map_real = maps_slice[0].astype(jnp.float32)[:, None, None]
    map_imag = maps_slice[1].astype(jnp.float32)[:, None, None]
    image_real = rounded[:, 0][:, :, :, None, :]
    image_imag = rounded[:, 1][:, :, :, None, :]
    coil_data = jnp.stack([map_real * image_real - map_imag * image_imag, map_real * image_imag + map_imag * image_real]).astype(jnp.bfloat16)
    spectrum = jnp.dot(forward_table, coil_data.reshape(2 * row_total, -1), preferred_element_type=jnp.float32).reshape(coil_data.shape)
    residual = (mask_rows[None, :, :, :, None, None] * (spectrum - kspace_slice.astype(jnp.float32))).astype(jnp.bfloat16)
    back_image = jnp.dot(adjoint_table, residual.reshape(2 * row_total, -1), preferred_element_type=jnp.float32).reshape(coil_data.shape)
    grad_real = lax.optimization_barrier(jnp.sum(map_real * back_image[0] + map_imag * back_image[1], axis=3))
    grad_imag = lax.optimization_barrier(jnp.sum(map_real * back_image[1] - map_imag * back_image[0], axis=3))
    return jnp.stack([grad_real, grad_imag], axis=1)

def reference(kspace, coil_maps, sampling_masks, start_image):
    forward_table, adjoint_table = transform_tables(NR)
    mask_rows = jnp.transpose(sampling_masks, (2, 1, 0)).astype(jnp.float32)
    kspace_slices = jnp.moveaxis(kspace, 4, 0)
    maps_slices = jnp.moveaxis(coil_maps, 2, 0)

    def one_slice(operands):
        image_slice, maps_slice, kspace_slice = operands
        return slice_gradient(image_slice, maps_slice, kspace_slice, mask_rows, forward_table, adjoint_table)
    current = start_image
    dual_field = jnp.zeros((4,) + start_image.shape, jnp.float32)
    for outer_step in range(OUTER):
        image_slices = jnp.moveaxis(current, 4, 0)
        gradient = jnp.moveaxis(lax.map(one_slice, (image_slices, maps_slices, kspace_slices)), 0, 4)
        anchor = current - DATA_STEP * gradient
        primal = anchor
        extrapolated = anchor
        for inner_step in range(TV_ITERS):
            dual_field = project(dual_field + DUAL_STEP * gradient_field(extrapolated), 2)
            updated = (primal + PRIMAL_STEP * divergence(dual_field) + PRIMAL_STEP * anchor) / (1.0 + PRIMAL_STEP)
            extrapolated = 2.0 * updated - primal
            primal = updated
        current = primal
    return (current, dual_field)
```

```python
import functools

import jax
import jax.numpy as jnp
import ml_dtypes
import numpy as np
from jax import lax
from jax.experimental import pallas as pl
from jax.experimental.pallas import tpu as pltpu
from jax.sharding import PartitionSpec as P

OUTER = 2
TV_ITERS = 3
STAGES = TV_ITERS + 2

DATA_STEP = 0.5
DUAL_STEP = 0.25
PRIMAL_STEP = 0.25
SMOOTH_WEIGHT = 0.3

MESH = pl.DeviceIdType.MESH
BF16 = jnp.bfloat16
F32 = jnp.float32


def transform_tables(length):
    position = np.arange(length, dtype=np.int64)
    phase_grid = (position[:, None] * position[None, :]) % length
    angles = phase_grid.astype(np.float32) * np.float32(2.0 * np.pi / length)
    norming = np.float32(1.0) / np.sqrt(np.float32(length))
    real_part = (np.cos(angles) * norming).astype(ml_dtypes.bfloat16)
    imag_part = (-np.sin(angles) * norming).astype(ml_dtypes.bfloat16)
    forward_table = np.block([[real_part, -imag_part], [imag_part, real_part]])
    adjoint_table = np.block([[real_part, imag_part], [-imag_part, real_part]])
    return forward_table, adjoint_table


def project(real_part, imag_part):
    factor = jnp.minimum(
        SMOOTH_WEIGHT * lax.rsqrt(real_part * real_part + imag_part * imag_part), 1.0
    )
    return real_part * factor, imag_part * factor


def kernel(
    sizes,
    kspace_hbm, maps_hbm, mask_ref, image_hbm, forward_hbm, adjoint_hbm,
    image_out, dual_out,
    kspace_raw, maps_raw, kspace_ref, maps_ref, forward_ref, adjoint_ref, masked_ref,
    gathered, coil_data, residual, partial, arrived,
    primal, anchor, bar, dual, rim_rows, rim_slices, halo_rows, halo_wide,
    load_sem, ag_send, ag_recv, rs_send, rs_recv, halo_send, halo_recv, out_sem,
):
    NR, NCOL, NC, ENC, COIL, CUTS, FRAME = sizes
    ROWS = NR // COIL
    me = lax.axis_index("coil")
    cut = lax.axis_index("cuts")
    frame = lax.axis_index("frame")
    my_rows = pl.ds(pl.multiple_of(me * ROWS, ROWS), ROWS)

    peers = [{"coil": lax.rem(me + d, COIL)} for d in range(1, COIL)]
    above, below = {"coil": lax.rem(me + COIL - 1, COIL)}, {"coil": lax.rem(me + 1, COIL)}
    before, behind = {"cuts": lax.rem(cut + CUTS - 1, CUTS)}, {"cuts": lax.rem(cut + 1, CUTS)}
    partner = {"frame": 1 - frame}

    def image_load(e, p):
        return pltpu.make_async_copy(
            image_hbm.at[:, p * ENC + e, 0, :], primal.at[e, p], load_sem.at[2 * e + p]
        )

    def plain_load(src, dst, i):
        return pltpu.make_async_copy(src, dst, load_sem.at[2 * ENC + i])

    loads = [
        plain_load(maps_hbm, maps_raw, 0),
        plain_load(forward_hbm, forward_ref, 1),
        plain_load(kspace_hbm, kspace_raw, 2),
        plain_load(adjoint_hbm, adjoint_ref, 3),
    ]
    for e in range(ENC):
        for p in range(2):
            image_load(e, p).start()
    for load in loads:
        load.start()

    barrier = pltpu.get_barrier_semaphore()
    greeted = peers + [before, behind, partner]
    for other in greeted:
        pl.semaphore_signal(barrier, inc=1, device_id=other, device_id_type=MESH)
    pl.semaphore_wait(barrier, len(greeted))

    def ag_copy(e, d):
        return pltpu.make_async_remote_copy(
            gathered.at[e, :, my_rows, :], gathered.at[e, :, my_rows, :],
            ag_send.at[e, d], ag_recv.at[e, d], device_id=peers[d], device_id_type=MESH,
        )

    def ag_wait(e, d):
        rows = pl.ds(pl.multiple_of(lax.rem(me + COIL - 1 - d, COIL) * ROWS, ROWS), ROWS)
        here = gathered.at[e, :, rows, :]
        pltpu.make_async_remote_copy(
            here, here, ag_send.at[e, d], ag_recv.at[e, d], device_id=peers[d], device_id_type=MESH
        ).wait_recv()

    def rs_copy(e, d):
        return pltpu.make_async_remote_copy(
            partial.at[e, peers[d]["coil"]], arrived.at[e, d],
            rs_send.at[e, d], rs_recv.at[e, d], device_id=peers[d], device_id_type=MESH,
        )

    def halo_copies(e, parity):
        plan = [
            (bar.at[e, :, pl.ds(ROWS - 8, 8), :], halo_rows.at[parity, e, 0], below),
            (bar.at[e, :, pl.ds(0, 8), :], halo_rows.at[parity, e, 1], above),
            (bar.at[e], halo_wide.at[parity, e, 0], behind),
            (bar.at[e], halo_wide.at[parity, e, 1], before),
            (bar.at[e], halo_wide.at[parity, e, 2], partner),
        ]
        return [
            pltpu.make_async_remote_copy(
                src, dst, halo_send.at[e, i], halo_recv.at[parity, e, i],
                device_id=to, device_id_type=MESH,
            )
            for i, (src, dst, to) in enumerate(plan)
        ]

    def out_copies(e):
        copies = []
        for p in range(2):
            copies.append((primal.at[e, p], image_out.at[:, p * ENC + e, 0, :]))
            for k in range(4):
                copies.append((dual.at[e, k, p], dual_out.at[k, :, p * ENC + e, 0, :]))
        return [
            pltpu.make_async_copy(src, dst, out_sem.at[e, i]) for i, (src, dst) in enumerate(copies)
        ]

    def send_rounded(e):
        for p in range(2):
            gathered[e, p, my_rows, :] = primal[e, p].astype(BF16)
        for d in range(COIL - 1):
            ag_copy(e, d).start()

    for e in range(ENC):
        for p in range(2):
            image_load(e, p).wait()
        send_rounded(e)

    row_id = lax.broadcasted_iota(jnp.int32, (256, 256), 0)
    col_id = lax.broadcasted_iota(jnp.int32, (256, 256), 1)
    source = jnp.where(row_id < 128, 2 * row_id, 2 * row_id - 255)
    sort_rows = jnp.where(col_id == source, 1.0, 0.0).astype(BF16)

    def sorted_pair(block):
        return jnp.dot(
            sort_rows, block.reshape(256, NCOL), preferred_element_type=F32
        ).astype(BF16)

    loads[0].wait()
    for p in range(2):
        def maps_part(i, carry):
            rows = pl.ds(pl.multiple_of(i * 128, 128), 128)
            both = sorted_pair(maps_raw[p, rows])
            maps_ref[p, 0, rows, :] = both[:128]
            maps_ref[p, 1, rows, :] = both[128:]
            return carry

        lax.fori_loop(0, NR // 128, maps_part, 0)
    loads[2].wait()
    for p in range(2):
        def kspace_part(i, carry):
            e, part = lax.rem(i, ENC), lax.div(i, ENC)
            rows = pl.ds(pl.multiple_of(part * 128, 128), 128)
            both = sorted_pair(kspace_raw[p, rows, e])
            kspace_ref[e, p, 0, rows, :] = both[:128]
            kspace_ref[e, p, 1, rows, :] = both[128:]
            return carry

        lax.fori_loop(0, ENC * NR // 128, kspace_part, 0)
    loads[3].wait()
    for e in range(ENC):
        sampled = mask_ref[e].astype(F32)
        masked_ref[e] = (adjoint_ref[...].astype(F32) * sampled).astype(BF16)
    dual[...] = jnp.zeros_like(dual)
    rim_rows[...] = jnp.zeros_like(rim_rows)
    rim_slices[...] = jnp.zeros_like(rim_slices)
    loads[1].wait()

    def data_stage(e):
        for d in range(COIL - 1):
            ag_wait(e, d)
        for c in range(NC):
            map_real, map_imag = maps_ref[0, c].astype(F32), maps_ref[1, c].astype(F32)
            image_real, image_imag = gathered[e, 0].astype(F32), gathered[e, 1].astype(F32)
            coil_data[c, :NR] = (map_real * image_real - map_imag * image_imag).astype(BF16)
            coil_data[c, NR:] = (map_real * image_imag + map_imag * image_real).astype(BF16)
            for p in range(2):
                spectrum = jnp.dot(
                    forward_ref[p * NR : (p + 1) * NR], coil_data[c], preferred_element_type=F32
                )
                residual[c, p * NR : (p + 1) * NR] = (
                    spectrum - kspace_ref[e, p, c].astype(F32)
                ).astype(BF16)
        for c in range(NC):
            map_real, map_imag = maps_ref[0, c].astype(F32), maps_ref[1, c].astype(F32)
            back_real = jnp.dot(masked_ref[e, :NR], residual[c], preferred_element_type=F32)
            back_imag = jnp.dot(masked_ref[e, NR:], residual[c], preferred_element_type=F32)
            grad_real = (map_real * back_real + map_imag * back_imag).reshape(COIL, ROWS, NCOL)
            grad_imag = (map_real * back_imag - map_imag * back_real).reshape(COIL, ROWS, NCOL)
            if c == 0:
                partial[e, :, 0], partial[e, :, 1] = grad_real, grad_imag
            else:
                partial[e, :, 0] += grad_real
                partial[e, :, 1] += grad_imag
        for d in range(COIL - 1):
            rs_copy(e, d).start()
        for d in range(COIL - 1):
            ag_copy(e, d).wait_send()

    def anchor_stage(e, turn):
        for d in range(COIL - 1):
            rs_copy(e, d).wait_recv()
        for p in range(2):
            total = partial[e, me, p]
            for d in range(COIL - 1):
                total = total + arrived[e, d, p]
            moved = primal[e, p] - DATA_STEP * total
            anchor[e, p] = moved
            primal[e, p] = moved
            bar[e, p] = moved
        for copy in halo_copies(e, lax.rem(turn, 2)):
            copy.start()
        for d in range(COIL - 1):
            rs_copy(e, d).wait_send()

    rows_at = lax.broadcasted_iota(jnp.int32, (ROWS, NCOL), 0)
    cols_at = lax.broadcasted_iota(jnp.int32, (ROWS, NCOL), 1)
    last_row = rows_at == ROWS - 1
    first_row = rows_at == 0
    row_keep = jnp.where(jnp.logical_and(last_row, me == COIL - 1), 0.0, DUAL_STEP)
    rim_keep = jnp.where(me == 0, 0.0, 1.0)
    slice_keep = jnp.where(cut == CUTS - 1, 0.0, DUAL_STEP)
    rim_slice_keep = jnp.where(cut == 0, 0.0, 1.0)
    col_keep = jnp.where(cols_at == NCOL - 1, 0.0, DUAL_STEP)
    col_back = jnp.where(cols_at == 0, 0.0, 1.0)

    def tv_stage(e, it, outer):
        parity = lax.rem(outer * TV_ITERS + it, 2)
        for copy in halo_copies(e, parity):
            copy.wait_recv()
        for copy in halo_copies(e, parity):
            copy.wait_send()
        x = [bar[e, p] for p in range(2)]
        spread = [None, None]

        def stepped(k, diffs):
            new = project(*[dual[e, k, p] + diffs[p] for p in range(2)])
            for p in range(2):
                dual[e, k, p] = new[p]
            return new

        rows = stepped(0, [
            row_keep * (jnp.where(last_row, halo_rows[parity, e, 1, p, 0:1, :], pltpu.roll(x[p], ROWS - 1, 0)) - x[p])
            for p in range(2)
        ])
        rim = project(*[
            rim_rows[e, p] + DUAL_STEP * (x[p][0:8] - halo_rows[parity, e, 0, p, 7:8, :])
            for p in range(2)
        ])
        for p in range(2):
            edge = rim[p] * rim_keep
            rim_rows[e, p] = edge
            spread[p] = rows[p] - jnp.where(first_row, edge[0:1], pltpu.roll(rows[p], 1, 0))
        cols = stepped(1, [col_keep * (pltpu.roll(x[p], NCOL - 1, 1) - x[p]) for p in range(2)])
        for p in range(2):
            spread[p] = spread[p] + (cols[p] - col_back * pltpu.roll(cols[p], 1, 1))
        cuts = stepped(2, [slice_keep * (halo_wide[parity, e, 1, p] - x[p]) for p in range(2)])
        rim = project(*[
            rim_slices[e, p] + DUAL_STEP * (x[p] - halo_wide[parity, e, 0, p]) for p in range(2)
        ])
        for p in range(2):
            edge = rim[p] * rim_slice_keep
            rim_slices[e, p] = edge
            spread[p] = spread[p] + (cuts[p] - edge)
        frames = stepped(3, [DUAL_STEP * (halo_wide[parity, e, 2, p] - x[p]) for p in range(2)])
        for p in range(2):
            spread[p] = spread[p] + 2.0 * frames[p]
            held = primal[e, p]
            updated = (held + PRIMAL_STEP * spread[p] + PRIMAL_STEP * anchor[e, p]) * (
                1.0 / (1.0 + PRIMAL_STEP)
            )
            primal[e, p] = updated
            bar[e, p] = 2.0 * updated - held

        @pl.when(it < TV_ITERS - 1)
        def _():
            for copy in halo_copies(e, 1 - parity):
                copy.start()

        @pl.when(jnp.logical_and(it == TV_ITERS - 1, outer < OUTER - 1))
        def _():
            send_rounded(e)

        @pl.when(jnp.logical_and(it == TV_ITERS - 1, outer == OUTER - 1))
        def _():
            for copy in out_copies(e):
                copy.start()

    def slot(t, carry):
        def one(i, carry):
            e = ENC - 1 - i
            at = t - e
            outer = lax.div(at, STAGES)
            stage = lax.rem(at, STAGES)
            active = jnp.logical_and(at >= 0, at < OUTER * STAGES)

            @pl.when(jnp.logical_and(active, stage == 0))
            def _():
                data_stage(e)

            @pl.when(jnp.logical_and(active, stage == 1))
            def _():
                anchor_stage(e, outer * TV_ITERS)

            @pl.when(jnp.logical_and(active, stage >= 2))
            def _():
                tv_stage(e, stage - 2, outer)

            return carry

        return lax.fori_loop(0, ENC, one, carry)

    lax.fori_loop(0, OUTER * STAGES + ENC - 1, slot, 0)

    for e in range(ENC):
        for copy in out_copies(e):
            copy.wait()


def solution(mesh):
    COIL, CUTS, FRAME = mesh.shape["coil"], mesh.shape["cuts"], mesh.shape["frame"]

    def shards(kspace, coil_maps, sampling_masks, start_image):
        _, NR, ENC, _, _, NC, NCOL = kspace.shape
        ROWS = start_image.shape[0]
        forward_table, adjoint_table = transform_tables(NR)
        masks = jnp.concatenate([sampling_masks[0], sampling_masks[0]], axis=-1)[:, None, :]
        hbm = pl.BlockSpec(memory_space=pltpu.HBM)
        vmem = pl.BlockSpec(memory_space=pltpu.VMEM)
        dma = pltpu.SemaphoreType.DMA
        image, dual = pl.pallas_call(
            functools.partial(kernel, (NR, NCOL, NC, ENC, COIL, CUTS, FRAME)),
            out_shape=(
                jax.ShapeDtypeStruct((ROWS, 2 * ENC, 1, NCOL), F32),
                jax.ShapeDtypeStruct((4, ROWS, 2 * ENC, 1, NCOL), F32),
            ),
            in_specs=[hbm, hbm, vmem, hbm, hbm, hbm],
            out_specs=(hbm, hbm),
            scratch_shapes=[
                pltpu.VMEM((2, NR, ENC, NC, NCOL), BF16),
                pltpu.VMEM((2, NR, NC, NCOL), BF16),
                pltpu.VMEM((ENC, 2, NC, NR, NCOL), BF16),
                pltpu.VMEM((2, NC, NR, NCOL), BF16),
                pltpu.VMEM((2 * NR, 2 * NR), BF16),
                pltpu.VMEM((2 * NR, 2 * NR), BF16),
                pltpu.VMEM((ENC, 2 * NR, 2 * NR), BF16),
                pltpu.VMEM((ENC, 2, NR, NCOL), BF16),
                pltpu.VMEM((NC, 2 * NR, NCOL), BF16),
                pltpu.VMEM((NC, 2 * NR, NCOL), BF16),
                pltpu.VMEM((ENC, COIL, 2, ROWS, NCOL), F32),
                pltpu.VMEM((ENC, COIL - 1, 2, ROWS, NCOL), F32),
                pltpu.VMEM((ENC, 2, ROWS, NCOL), F32),
                pltpu.VMEM((ENC, 2, ROWS, NCOL), F32),
                pltpu.VMEM((ENC, 2, ROWS, NCOL), F32),
                pltpu.VMEM((ENC, 4, 2, ROWS, NCOL), F32),
                pltpu.VMEM((ENC, 2, 8, NCOL), F32),
                pltpu.VMEM((ENC, 2, ROWS, NCOL), F32),
                pltpu.VMEM((2, ENC, 2, 2, 8, NCOL), F32),
                pltpu.VMEM((2, ENC, 3, 2, ROWS, NCOL), F32),
                dma((2 * ENC + 4,)),
                dma((ENC, COIL - 1)),
                dma((ENC, COIL - 1)),
                dma((ENC, COIL - 1)),
                dma((ENC, COIL - 1)),
                dma((ENC, 5)),
                dma((2, ENC, 5)),
                dma((ENC, 10)),
            ],
            compiler_params=pltpu.CompilerParams(
                collective_id=0, has_side_effects=True, vmem_limit_bytes=40 << 20
            ),
            name="sense_tv",
        )(
            kspace.reshape(2, NR, ENC, NC, NCOL),
            coil_maps.reshape(2, NR, NC, NCOL),
            masks,
            start_image.reshape(ROWS, 2 * ENC, 1, NCOL),
            jnp.asarray(forward_table),
            jnp.asarray(adjoint_table),
        )
        return (
            image.reshape(ROWS, 2, ENC, 1, 1, NCOL),
            dual.reshape(4, ROWS, 2, ENC, 1, 1, NCOL),
        )

    return jax.shard_map(
        shards,
        mesh=mesh,
        in_specs=(
            P(None, None, None, "frame", "cuts", "coil", None),
            P(None, None, "cuts", "coil", None),
            P("frame", None, None),
            P("coil", None, None, "frame", "cuts", None),
        ),
        out_specs=(
            P("coil", None, None, "frame", "cuts", None),
            P(None, "coil", None, None, "frame", "cuts", None),
        ),
        check_vma=False,
    )
```

```python
import functools

import jax
import jax.numpy as jnp
import ml_dtypes
import numpy as np
from jax import lax
from jax.experimental import pallas as pl
from jax.experimental.pallas import tpu as pltpu
from jax.sharding import PartitionSpec as P

OUTER = 2
TV_ITERS = 3
STAGES = TV_ITERS + 4

DATA_STEP = 0.5
DUAL_STEP = 0.25
PRIMAL_STEP = 0.25
SMOOTH_WEIGHT = 0.3

MESH = pl.DeviceIdType.MESH
BF16 = jnp.bfloat16
F32 = jnp.float32


def transform_tables(length):
    position = np.arange(length, dtype=np.int64)
    phase_grid = (position[:, None] * position[None, :]) % length
    angles = phase_grid.astype(np.float32) * np.float32(2.0 * np.pi / length)
    norming = np.float32(1.0) / np.sqrt(np.float32(length))
    real_part = (np.cos(angles) * norming).astype(ml_dtypes.bfloat16)
    imag_part = (-np.sin(angles) * norming).astype(ml_dtypes.bfloat16)
    forward_table = np.block([[real_part, -imag_part], [imag_part, real_part]])
    adjoint_table = np.block([[real_part, imag_part], [-imag_part, real_part]])
    return forward_table, adjoint_table


def project(real_part, imag_part):
    factor = jnp.minimum(
        SMOOTH_WEIGHT * lax.rsqrt(real_part * real_part + imag_part * imag_part), 1.0
    )
    return real_part * factor, imag_part * factor


def kernel(
    sizes,
    kspace_hbm, maps_hbm, mask_hbm, image_hbm, forward_hbm, adjoint_hbm,
    image_out, dual_out,
    kspace_raw, maps_raw, kspace_ref, maps_ref, forward_ref, adjoint_ref, masked_ref,
    mask_ref, image_ref, rounded, gathered, coil_data, residual, partial, coded, unit, arrived, units,
    primal, anchor, bar, dual, rim_rows, rim_slices, edges, halo_rows, halo_wide,
    load_sem, first_send, first_recv, start_send, start_recv, ag_send, ag_recv,
    rs_send, rs_recv, unit_send, unit_recv, halo_send, halo_recv, out_send, out_recv,
):
    NR, NCOL, NC, ENC, COIL, CUTS, FRAME = sizes
    ROWS = NR // COIL
    PART = ROWS // FRAME
    LOW = COIL // 4
    WIDE = LOW * FRAME
    BLOCKS = 4 * WIDE
    me = lax.axis_index("coil")
    cut = lax.axis_index("cuts")
    frame = lax.axis_index("frame")
    my_y, my_x = lax.div(me, LOW), frame * LOW + lax.rem(me, LOW)

    def place(y, x):
        return {"coil": y * LOW + lax.rem(x, LOW), "frame": lax.div(x, LOW)}

    def turned(y, x):
        return jnp.where(lax.rem(y, 2) == 0, x, WIDE - 1 - x)

    def block_of(y, x):
        return y * WIDE + turned(y, x)

    def holder(block):
        y = lax.div(block, WIDE)
        return y, turned(y, lax.rem(block, WIDE))

    mine = block_of(my_y, my_x)
    my_block = pl.ds(pl.multiple_of(mine * PART, PART), PART)
    my_rows = pl.ds(pl.multiple_of(me * ROWS, ROWS), ROWS)
    my_place = frame * COIL + me

    offsets = [(dy, dx) for dy in range(4) for dx in range(WIDE) if (dy, dx) != (0, 0)]
    PEERS = len(offsets)
    there = [(lax.rem(my_y + dy, 4), lax.rem(my_x + dx, WIDE)) for dy, dx in offsets]
    origin = [
        (lax.rem(my_y + 4 - dy, 4), lax.rem(my_x + WIDE - dx, WIDE)) for dy, dx in offsets
    ]
    above = place(*holder(lax.rem(mine + BLOCKS - 1, BLOCKS)))
    below = place(*holder(lax.rem(mine + 1, BLOCKS)))
    before, behind = {"cuts": lax.rem(cut + CUTS - 1, CUTS)}, {"cuts": lax.rem(cut + 1, CUTS)}

    def image_load(e, p):
        return pltpu.make_async_copy(
            image_hbm.at[:, p * ENC + e, 0, :], image_ref.at[e, p], load_sem.at[2 * e + p]
        )

    def plain_load(src, dst, i):
        return pltpu.make_async_copy(src, dst, load_sem.at[2 * ENC + i])

    loads = [
        plain_load(maps_hbm, maps_raw, 0),
        plain_load(forward_hbm, forward_ref, 1),
        plain_load(kspace_hbm, kspace_raw, 2),
        plain_load(adjoint_hbm, adjoint_ref, 3),
        plain_load(mask_hbm, mask_ref, 4),
    ]
    for e in range(ENC):
        for p in range(2):
            image_load(e, p).start()
    for load in loads:
        load.start()

    barrier = pltpu.get_barrier_semaphore()
    greeted = [place(*t) for t in there] + [before, behind]
    for other in greeted:
        pl.semaphore_signal(barrier, inc=1, device_id=other, device_id_type=MESH)
    pl.semaphore_wait(barrier, len(greeted))

    def first_copy(e, d):
        other = {"coil": lax.rem(me + 1 + d, COIL)}
        return pltpu.make_async_remote_copy(
            gathered.at[e, :, my_rows, :], gathered.at[e, :, my_rows, :],
            first_send.at[e, d], first_recv.at[e, d], device_id=other, device_id_type=MESH,
        )

    def first_wait(e, d):
        rows = pl.ds(pl.multiple_of(lax.rem(me + COIL - 1 - d, COIL) * ROWS, ROWS), ROWS)
        here = gathered.at[e, :, rows, :]
        pltpu.make_async_remote_copy(
            here, here, first_send.at[e, d], first_recv.at[e, d],
            device_id={"coil": lax.rem(me + 1 + d, COIL)}, device_id_type=MESH,
        ).wait_recv()

    def start_block(k):
        return my_y * WIDE + lax.rem(me, LOW) * FRAME + k

    def start_remote(k):
        return pltpu.make_async_remote_copy(
            image_ref.at[:, :, pl.ds(k * PART, PART), :], primal.at[frame],
            start_send.at[k], start_recv.at[frame],
            device_id=place(*holder(start_block(k))), device_id_type=MESH,
        )

    def start_local(k):
        return pltpu.make_async_copy(
            image_ref.at[:, :, pl.ds(k * PART, PART), :], primal.at[frame], start_send.at[k]
        )

    def ag_copy(e, d):
        return pltpu.make_async_remote_copy(
            rounded.at[e, lax.div(there[d][1], LOW)], gathered.at[e, :, my_block, :],
            ag_send.at[e, d], ag_recv.at[e, d],
            device_id=place(*there[d]), device_id_type=MESH,
        )

    def ag_wait(e, d):
        rows = pl.ds(pl.multiple_of(block_of(*origin[d]) * PART, PART), PART)
        here = gathered.at[e, :, rows, :]
        pltpu.make_async_remote_copy(
            here, here, ag_send.at[e, d], ag_recv.at[e, d],
            device_id=place(*there[d]), device_id_type=MESH,
        ).wait_recv()

    def rs_copy(e, d):
        return pltpu.make_async_remote_copy(
            coded.at[e, block_of(*there[d])], arrived.at[e, my_place],
            rs_send.at[e, d], rs_recv.at[e, d],
            device_id=place(*there[d]), device_id_type=MESH,
        )

    def unit_copy(e, d):
        return pltpu.make_async_remote_copy(
            unit.at[e], units.at[e, my_place], unit_send.at[e, d], unit_recv.at[e, d],
            device_id=place(*there[d]), device_id_type=MESH,
        )

    def halo_copies(e, parity):
        plan = [
            (edges.at[e, 0], halo_rows.at[parity, e, 0], below),
            (edges.at[e, 1], halo_rows.at[parity, e, 1], above),
            (bar.at[e], halo_wide.at[parity, e, 0], behind),
            (bar.at[e], halo_wide.at[parity, e, 1], before),
        ]
        return [
            pltpu.make_async_remote_copy(
                src, dst, halo_send.at[e, i], halo_recv.at[parity, e, i],
                device_id=to, device_id_type=MESH,
            )
            for i, (src, dst, to) in enumerate(plan)
        ]

    my_turn = turned(my_y, my_x)
    my_half = lax.rem(my_turn, FRAME)

    def owner(f):
        return my_y, f * LOW + lax.div(my_turn, FRAME)

    def out_plan(e, f, half):
        rows = pl.ds(pl.multiple_of(half * PART, PART), PART)
        plan = []
        for p in range(2):
            plan.append((primal.at[f, e, p], image_out.at[rows, p * ENC + e, 0, :]))
            for k in range(4):
                plan.append((dual.at[e, k, f, p], dual_out.at[k, rows, p * ENC + e, 0, :]))
        return plan

    def out_remote(e, f):
        return [
            pltpu.make_async_remote_copy(
                src, dst, out_send.at[e, f, i], out_recv.at[e, my_half, i],
                device_id=place(*owner(f)), device_id_type=MESH,
            )
            for i, (src, dst) in enumerate(out_plan(e, f, my_half))
        ]

    def out_local(e, f):
        return [
            pltpu.make_async_copy(src, dst, out_send.at[e, f, i])
            for i, (src, dst) in enumerate(out_plan(e, f, my_half))
        ]

    def out_arrival(e, half):
        return [
            pltpu.make_async_remote_copy(
                dst, dst, out_send.at[e, 0, i], out_recv.at[e, half, i],
                device_id=before, device_id_type=MESH,
            )
            for i, (src, dst) in enumerate(out_plan(e, 0, half))
        ]

    for e in range(ENC):
        for p in range(2):
            image_load(e, p).wait()
            gathered[e, p, my_rows, :] = image_ref[e, p].astype(BF16)
        for d in range(COIL - 1):
            first_copy(e, d).start()
    for k in range(FRAME):
        y, x = holder(start_block(k))

        @pl.when(x != my_x)
        def _():
            start_remote(k).start()

        @pl.when(x == my_x)
        def _():
            start_local(k).start()

    row_id = lax.broadcasted_iota(jnp.int32, (256, 256), 0)
    col_id = lax.broadcasted_iota(jnp.int32, (256, 256), 1)
    source = jnp.where(row_id < 128, 2 * row_id, 2 * row_id - 255)
    sort_rows = jnp.where(col_id == source, 1.0, 0.0).astype(BF16)

    def sorted_pair(block):
        return jnp.dot(
            sort_rows, block.reshape(256, NCOL), preferred_element_type=F32
        ).astype(BF16)

    loads[0].wait()
    for p in range(2):
        def maps_part(i, carry):
            rows = pl.ds(pl.multiple_of(i * 128, 128), 128)
            both = sorted_pair(maps_raw[p, rows])
            maps_ref[p, 0, rows, :] = both[:128]
            maps_ref[p, 1, rows, :] = both[128:]
            return carry

        lax.fori_loop(0, NR // 128, maps_part, 0)
    loads[2].wait()
    for p in range(2):
        def kspace_part(i, carry):
            e, part = lax.rem(i, ENC), lax.div(i, ENC)
            rows = pl.ds(pl.multiple_of(part * 128, 128), 128)
            both = sorted_pair(kspace_raw[p, rows, e])
            kspace_ref[e, p, 0, rows, :] = both[:128]
            kspace_ref[e, p, 1, rows, :] = both[128:]
            return carry

        lax.fori_loop(0, ENC * NR // 128, kspace_part, 0)
    loads[3].wait()
    loads[4].wait()

    def mask_part(i, carry):
        e, part = lax.rem(i, ENC), lax.div(i, ENC)
        rows = pl.ds(pl.multiple_of(part * 64, 64), 64)
        sampled = mask_ref[e].astype(F32)
        for p in range(2):
            columns = pl.ds(p * NR, NR)
            masked_ref[e, rows, columns] = (
                adjoint_ref[rows, columns].astype(F32) * sampled
            ).astype(BF16)
        return carry

    lax.fori_loop(0, ENC * 2 * NR // 64, mask_part, 0)
    dual[...] = jnp.zeros_like(dual)
    rim_rows[...] = jnp.zeros_like(rim_rows)
    rim_slices[...] = jnp.zeros_like(rim_slices)
    edges[...] = jnp.zeros_like(edges)
    loads[1].wait()
    for k in range(FRAME):
        y, x = holder(start_block(k))

        @pl.when(x != my_x)
        def _():
            start_remote(k).wait_send()

        @pl.when(x == my_x)
        def _():
            start_local(k).wait()

    for f in range(FRAME):
        @pl.when(owner(f)[1] != my_x)
        def _():
            pltpu.make_async_remote_copy(
                primal.at[f], primal.at[f], start_send.at[0], start_recv.at[f],
                device_id=before, device_id_type=MESH,
            ).wait_recv()

    def data_stage(e, outer):
        @pl.when(outer == 0)
        def _():
            for d in range(COIL - 1):
                first_wait(e, d)

        @pl.when(outer != 0)
        def _():
            for d in range(PEERS):
                ag_wait(e, d)

        for c in range(NC):
            map_real, map_imag = maps_ref[0, c].astype(F32), maps_ref[1, c].astype(F32)
            image_real, image_imag = gathered[e, 0].astype(F32), gathered[e, 1].astype(F32)
            coil_data[c, :NR] = (map_real * image_real - map_imag * image_imag).astype(BF16)
            coil_data[c, NR:] = (map_real * image_imag + map_imag * image_real).astype(BF16)
            for p in range(2):
                spectrum = jnp.dot(
                    forward_ref[p * NR : (p + 1) * NR], coil_data[c], preferred_element_type=F32
                )
                residual[c, p * NR : (p + 1) * NR] = (
                    spectrum - kspace_ref[e, p, c].astype(F32)
                ).astype(BF16)
        for c in range(NC):
            map_real, map_imag = maps_ref[0, c].astype(F32), maps_ref[1, c].astype(F32)
            back_real = jnp.dot(masked_ref[e, :NR], residual[c], preferred_element_type=F32)
            back_imag = jnp.dot(masked_ref[e, NR:], residual[c], preferred_element_type=F32)
            grad_real = (map_real * back_real + map_imag * back_imag).reshape(BLOCKS, PART, NCOL)
            grad_imag = (map_real * back_imag - map_imag * back_real).reshape(BLOCKS, PART, NCOL)
            if c == 0:
                partial[:, 0], partial[:, 1] = grad_real, grad_imag
            else:
                partial[:, 0] += grad_real
                partial[:, 1] += grad_imag
        top = jnp.max(jnp.abs(partial[...]), axis=(0, 1, 2, 3), keepdims=True)[0, 0]
        step = jnp.broadcast_to(jnp.maximum(top, 1e-30) * (1.0 / 32000.0), (1, NCOL))
        unit[e] = step
        coded[e] = jnp.round(partial[...] * (1.0 / step)).astype(jnp.int32).astype(jnp.int16)
        for d in range(PEERS):
            unit_copy(e, d).start()
            rs_copy(e, d).start()
        units[e, my_place] = step
        arrived[e, my_place] = coded[e, mine]

        @pl.when(outer == 0)
        def _():
            for d in range(COIL - 1):
                first_copy(e, d).wait_send()

        @pl.when(outer != 0)
        def _():
            for d in range(PEERS):
                ag_copy(e, d).wait_send()

    def publish(e, x, parity):
        for f in range(FRAME):
            for p in range(2):
                bar[e, f, p] = x[f][p]
                i = 2 * f + p
                edges[e, 0, i : i + 1, :] = x[f][p][PART - 1 : PART]
                edges[e, 1, i : i + 1, :] = x[f][p][0:1]
        for copy in halo_copies(e, parity):
            copy.start()

    def anchor_stage(e, outer):
        for d in range(PEERS):
            unit_copy(e, d).wait_recv()
            rs_copy(e, d).wait_recv()
        x = [[None, None], [None, None]]
        for f in range(FRAME):
            for p in range(2):
                total = jnp.zeros((PART, NCOL), F32)
                for c in range(f * COIL, f * COIL + COIL):
                    total = total + arrived[e, c, p].astype(F32) * units[e, c]
                x[f][p] = primal[f, e, p] - DATA_STEP * total
                anchor[e, f, p] = x[f][p]
                primal[f, e, p] = x[f][p]
        publish(e, x, lax.rem(outer * TV_ITERS, 2))
        for d in range(PEERS):
            unit_copy(e, d).wait_send()
            rs_copy(e, d).wait_send()

    rows_at = lax.broadcasted_iota(jnp.int32, (PART, NCOL), 0)
    cols_at = lax.broadcasted_iota(jnp.int32, (PART, NCOL), 1)
    last_row = rows_at == PART - 1
    first_row = rows_at == 0
    row_keep = jnp.where(jnp.logical_and(last_row, mine == BLOCKS - 1), 0.0, DUAL_STEP)
    rim_keep = jnp.where(mine == 0, 0.0, 1.0)
    slice_keep = jnp.where(cut == CUTS - 1, 0.0, DUAL_STEP)
    rim_slice_keep = jnp.where(cut == 0, 0.0, 1.0)
    col_keep = jnp.where(cols_at == NCOL - 1, 0.0, DUAL_STEP)
    col_back = jnp.where(cols_at == 0, 0.0, 1.0)

    def tv_stage(e, it, outer):
        parity = lax.rem(outer * TV_ITERS + it, 2)
        for copy in halo_copies(e, parity):
            copy.wait_recv()
        for copy in halo_copies(e, parity):
            copy.wait_send()
        both = [[bar[e, f, p] for p in range(2)] for f in range(FRAME)]
        swing = project(*[
            dual[e, 3, 0, p] + DUAL_STEP * (both[1][p] - both[0][p]) for p in range(2)
        ])
        fresh = [[None, None], [None, None]]
        for p in range(2):
            dual[e, 3, 0, p] = swing[p]
            dual[e, 3, 1, p] = -swing[p]
        for f in range(FRAME):
            x = both[f]

            def stepped(k, diffs):
                new = project(*[dual[e, k, f, p] + diffs[p] for p in range(2)])
                for p in range(2):
                    dual[e, k, f, p] = new[p]
                return new

            after = [halo_rows[parity, e, 1, 2 * f + p : 2 * f + p + 1, :] for p in range(2)]
            prior = [halo_rows[parity, e, 0, 2 * f + p : 2 * f + p + 1, :] for p in range(2)]
            rows = stepped(0, [
                row_keep * (jnp.where(last_row, after[p], pltpu.roll(x[p], PART - 1, 0)) - x[p])
                for p in range(2)
            ])
            rim = project(*[
                rim_rows[e, f, p] + DUAL_STEP * (x[p][0:8] - prior[p]) for p in range(2)
            ])
            spread = [None, None]
            for p in range(2):
                edge = rim[p] * rim_keep
                rim_rows[e, f, p] = edge
                spread[p] = rows[p] - jnp.where(first_row, edge[0:1], pltpu.roll(rows[p], 1, 0))
            cols = stepped(1, [col_keep * (pltpu.roll(x[p], NCOL - 1, 1) - x[p]) for p in range(2)])
            for p in range(2):
                spread[p] = spread[p] + (cols[p] - col_back * pltpu.roll(cols[p], 1, 1))
            cuts = stepped(2, [slice_keep * (halo_wide[parity, e, 1, f, p] - x[p]) for p in range(2)])
            rim = project(*[
                rim_slices[e, f, p] + DUAL_STEP * (x[p] - halo_wide[parity, e, 0, f, p])
                for p in range(2)
            ])
            for p in range(2):
                edge = rim[p] * rim_slice_keep
                rim_slices[e, f, p] = edge
                spread[p] = spread[p] + (cuts[p] - edge)
            for p in range(2):
                spread[p] = spread[p] + (2.0 - 4.0 * f) * swing[p]
                held = primal[f, e, p]
                updated = (held + PRIMAL_STEP * spread[p] + PRIMAL_STEP * anchor[e, f, p]) * (
                    1.0 / (1.0 + PRIMAL_STEP)
                )
                primal[f, e, p] = updated
                fresh[f][p] = 2.0 * updated - held

        @pl.when(it < TV_ITERS - 1)
        def _():
            publish(e, fresh, 1 - parity)

        @pl.when(jnp.logical_and(it == TV_ITERS - 1, outer < OUTER - 1))
        def _():
            for f in range(FRAME):
                for p in range(2):
                    rounded[e, f, p] = primal[f, e, p].astype(BF16)
            for d in range(PEERS):
                ag_copy(e, d).start()
            for p in range(2):
                gathered[e, p, my_block, :] = rounded[e, frame, p]

        @pl.when(jnp.logical_and(it == TV_ITERS - 1, outer == OUTER - 1))
        def _():
            for f in range(FRAME):
                @pl.when(owner(f)[1] != my_x)
                def _():
                    for copy in out_remote(e, f):
                        copy.start()

                @pl.when(owner(f)[1] == my_x)
                def _():
                    for copy in out_local(e, f):
                        copy.start()

    def slot(t, carry):
        def one(i, carry):
            e = ENC - 1 - i
            at = t - e
            outer = lax.div(at, STAGES)
            stage = lax.rem(at, STAGES)
            active = jnp.logical_and(at >= 0, at < OUTER * STAGES)

            @pl.when(jnp.logical_and(active, stage == 0))
            def _():
                data_stage(e, outer)

            @pl.when(jnp.logical_and(active, stage == 2))
            def _():
                anchor_stage(e, outer)

            @pl.when(jnp.logical_and(active, jnp.logical_and(stage >= 3, stage < 3 + TV_ITERS)))
            def _():
                tv_stage(e, stage - 3, outer)

            return carry

        return lax.fori_loop(0, ENC, one, carry)

    lax.fori_loop(0, OUTER * STAGES + ENC - 1, slot, 0)

    def finish(e, carry):
        for f in range(FRAME):
            @pl.when(owner(f)[1] != my_x)
            def _():
                for copy in out_remote(e, f):
                    copy.wait_send()

            @pl.when(owner(f)[1] == my_x)
            def _():
                for copy in out_local(e, f):
                    copy.wait()

        for half in range(FRAME):
            @pl.when(holder(start_block(half))[1] != my_x)
            def _():
                for copy in out_arrival(e, half):
                    copy.wait_recv()

        return carry

    lax.fori_loop(0, ENC, finish, 0)


def solution(mesh):
    COIL, CUTS, FRAME = mesh.shape["coil"], mesh.shape["cuts"], mesh.shape["frame"]

    def shards(kspace, coil_maps, sampling_masks, start_image):
        _, NR, ENC, _, _, NC, NCOL = kspace.shape
        ROWS = start_image.shape[0]
        PART = ROWS // FRAME
        peers = FRAME * COIL - 1
        forward_table, adjoint_table = transform_tables(NR)
        hbm = pl.BlockSpec(memory_space=pltpu.HBM)
        dma = pltpu.SemaphoreType.DMA
        image, dual = pl.pallas_call(
            functools.partial(kernel, (NR, NCOL, NC, ENC, COIL, CUTS, FRAME)),
            out_shape=(
                jax.ShapeDtypeStruct((ROWS, 2 * ENC, 1, NCOL), F32),
                jax.ShapeDtypeStruct((4, ROWS, 2 * ENC, 1, NCOL), F32),
            ),
            in_specs=[hbm] * 6,
            out_specs=(hbm, hbm),
            scratch_shapes=[
                pltpu.VMEM((2, NR, ENC, NC, NCOL), BF16),
                pltpu.VMEM((2, NR, NC, NCOL), BF16),
                pltpu.VMEM((ENC, 2, NC, NR, NCOL), BF16),
                pltpu.VMEM((2, NC, NR, NCOL), BF16),
                pltpu.VMEM((2 * NR, 2 * NR), BF16),
                pltpu.VMEM((2 * NR, 2 * NR), BF16),
                pltpu.VMEM((ENC, 2 * NR, 2 * NR), BF16),
                pltpu.VMEM((ENC, 1, NR), jnp.int32),
                pltpu.VMEM((ENC, 2, ROWS, NCOL), F32),
                pltpu.VMEM((ENC, FRAME, 2, PART, NCOL), BF16),
                pltpu.VMEM((ENC, 2, NR, NCOL), BF16),
                pltpu.VMEM((NC, 2 * NR, NCOL), BF16),
                pltpu.VMEM((NC, 2 * NR, NCOL), BF16),
                pltpu.VMEM((NR // PART, 2, PART, NCOL), F32),
                pltpu.VMEM((ENC, NR // PART, 2, PART, NCOL), jnp.int16),
                pltpu.VMEM((ENC, 1, NCOL), F32),
                pltpu.VMEM((ENC, FRAME * COIL, 2, PART, NCOL), jnp.int16),
                pltpu.VMEM((ENC, FRAME * COIL, 1, NCOL), F32),
                pltpu.VMEM((FRAME, ENC, 2, PART, NCOL), F32),
                pltpu.VMEM((ENC, FRAME, 2, PART, NCOL), F32),
                pltpu.VMEM((ENC, FRAME, 2, PART, NCOL), F32),
                pltpu.VMEM((ENC, 4, FRAME, 2, PART, NCOL), F32),
                pltpu.VMEM((ENC, FRAME, 2, 8, NCOL), F32),
                pltpu.VMEM((ENC, FRAME, 2, PART, NCOL), F32),
                pltpu.VMEM((ENC, 2, 8, NCOL), F32),
                pltpu.VMEM((2, ENC, 2, 8, NCOL), F32),
                pltpu.VMEM((2, ENC, 2, FRAME, 2, PART, NCOL), F32),
                dma((2 * ENC + 5,)),
                dma((ENC, COIL - 1)),
                dma((ENC, COIL - 1)),
                dma((FRAME,)),
                dma((FRAME,)),
                dma((ENC, peers)),
                dma((ENC, peers)),
                dma((ENC, peers)),
                dma((ENC, peers)),
                dma((ENC, peers)),
                dma((ENC, peers)),
                dma((ENC, 4)),
                dma((2, ENC, 4)),
                dma((ENC, FRAME, 10)),
                dma((ENC, FRAME, 10)),
            ],
            compiler_params=pltpu.CompilerParams(
                collective_id=0, has_side_effects=True, vmem_limit_bytes=60 << 20
            ),
            name="sense_tv",
        )(
            kspace.reshape(2, NR, ENC, NC, NCOL),
            coil_maps.reshape(2, NR, NC, NCOL),
            sampling_masks.reshape(ENC, 1, NR),
            start_image.reshape(ROWS, 2 * ENC, 1, NCOL),
            jnp.asarray(forward_table),
            jnp.asarray(adjoint_table),
        )
        return (
            image.reshape(ROWS, 2, ENC, 1, 1, NCOL),
            dual.reshape(4, ROWS, 2, ENC, 1, 1, NCOL),
        )

    return jax.shard_map(
        shards,
        mesh=mesh,
        in_specs=(
            P(None, None, None, "frame", "cuts", "coil", None),
            P(None, None, "cuts", "coil", None),
            P("frame", None, None),
            P("coil", None, None, "frame", "cuts", None),
        ),
        out_specs=(
            P("coil", None, None, "frame", "cuts", None),
            P(None, "coil", None, None, "frame", "cuts", None),
        ),
        check_vma=False,
    )
```

```python
import functools

import jax
import jax.numpy as jnp
import ml_dtypes
import numpy as np
from jax import lax
from jax.experimental import pallas as pl
from jax.experimental.pallas import tpu as pltpu
from jax.sharding import PartitionSpec as P

OUTER = 2
TV_ITERS = 3
STAGES = TV_ITERS + 4

DATA_STEP = 0.5
DUAL_STEP = 0.25
PRIMAL_STEP = 0.25
SMOOTH_WEIGHT = 0.3

MESH = pl.DeviceIdType.MESH
BF16 = jnp.bfloat16
F32 = jnp.float32
I16 = jnp.int16
CODES = 32000.0


def transform_tables(length):
    position = np.arange(length, dtype=np.int64)
    phase_grid = (position[:, None] * position[None, :]) % length
    angles = phase_grid.astype(np.float32) * np.float32(2.0 * np.pi / length)
    norming = np.float32(1.0) / np.sqrt(np.float32(length))
    real_part = (np.cos(angles) * norming).astype(ml_dtypes.bfloat16)
    imag_part = (-np.sin(angles) * norming).astype(ml_dtypes.bfloat16)
    forward_table = np.block([[real_part, -imag_part], [imag_part, real_part]])
    adjoint_table = np.block([[real_part, imag_part], [-imag_part, real_part]])
    return forward_table, adjoint_table


def coded_as(values, per_unit):
    return jnp.round(values * per_unit).astype(jnp.int32).astype(I16)


def project(real_part, imag_part):
    factor = jnp.minimum(
        SMOOTH_WEIGHT * lax.rsqrt(real_part * real_part + imag_part * imag_part), 1.0
    )
    return real_part * factor, imag_part * factor


def kernel(
    sizes,
    kspace_hbm, maps_hbm, mask_hbm, image_hbm, forward_hbm, adjoint_hbm,
    coded_out, unit_out,
    kspace_raw, maps_raw, kspace_ref, maps_ref, forward_ref, adjoint_ref, masked_ref,
    mask_ref, image_ref, rounded, gathered, coil_data, residual, partial, coded, unit, arrived, units,
    primal, anchor, bar, dual, rim_rows, rim_slices, edges, halo_rows, halo_wide,
    last, last_unit,
    load_sem, first_send, first_recv, start_send, start_recv, ag_send, ag_recv,
    rs_send, rs_recv, unit_send, unit_recv, halo_send, halo_recv, out_send, out_recv,
):
    NR, NCOL, NC, ENC, COIL, CUTS, FRAME = sizes
    ROWS = NR // COIL
    PART = ROWS // FRAME
    LOW = COIL // 4
    WIDE = LOW * FRAME
    BLOCKS = 4 * WIDE
    me = lax.axis_index("coil")
    cut = lax.axis_index("cuts")
    frame = lax.axis_index("frame")
    my_y, my_x = lax.div(me, LOW), frame * LOW + lax.rem(me, LOW)

    def place(y, x):
        return {"coil": y * LOW + lax.rem(x, LOW), "frame": lax.div(x, LOW)}

    def turned(y, x):
        return jnp.where(lax.rem(y, 2) == 0, x, WIDE - 1 - x)

    def block_of(y, x):
        return y * WIDE + turned(y, x)

    def holder(block):
        y = lax.div(block, WIDE)
        return y, turned(y, lax.rem(block, WIDE))

    mine = block_of(my_y, my_x)
    my_block = pl.ds(pl.multiple_of(mine * PART, PART), PART)
    my_rows = pl.ds(pl.multiple_of(me * ROWS, ROWS), ROWS)
    my_place = frame * COIL + me

    offsets = [(dy, dx) for dy in range(4) for dx in range(WIDE) if (dy, dx) != (0, 0)]
    PEERS = len(offsets)
    there = [(lax.rem(my_y + dy, 4), lax.rem(my_x + dx, WIDE)) for dy, dx in offsets]
    origin = [
        (lax.rem(my_y + 4 - dy, 4), lax.rem(my_x + WIDE - dx, WIDE)) for dy, dx in offsets
    ]
    above = place(*holder(lax.rem(mine + BLOCKS - 1, BLOCKS)))
    below = place(*holder(lax.rem(mine + 1, BLOCKS)))
    before, behind = {"cuts": lax.rem(cut + CUTS - 1, CUTS)}, {"cuts": lax.rem(cut + 1, CUTS)}

    def image_load(e, p):
        return pltpu.make_async_copy(
            image_hbm.at[:, p * ENC + e, 0, :], image_ref.at[e, p], load_sem.at[2 * e + p]
        )

    def plain_load(src, dst, i):
        return pltpu.make_async_copy(src, dst, load_sem.at[2 * ENC + i])

    loads = [
        plain_load(maps_hbm, maps_raw, 0),
        plain_load(forward_hbm, forward_ref, 1),
        plain_load(kspace_hbm, kspace_raw, 2),
        plain_load(adjoint_hbm, adjoint_ref, 3),
        plain_load(mask_hbm, mask_ref, 4),
    ]
    for e in range(ENC):
        for p in range(2):
            image_load(e, p).start()
    for load in loads:
        load.start()

    barrier = pltpu.get_barrier_semaphore()
    greeted = [place(*t) for t in there] + [before, behind]
    for other in greeted:
        pl.semaphore_signal(barrier, inc=1, device_id=other, device_id_type=MESH)
    pl.semaphore_wait(barrier, len(greeted))

    def first_copy(e, d):
        other = {"coil": lax.rem(me + 1 + d, COIL)}
        return pltpu.make_async_remote_copy(
            gathered.at[e, :, my_rows, :], gathered.at[e, :, my_rows, :],
            first_send.at[e, d], first_recv.at[e, d], device_id=other, device_id_type=MESH,
        )

    def first_wait(e, d):
        rows = pl.ds(pl.multiple_of(lax.rem(me + COIL - 1 - d, COIL) * ROWS, ROWS), ROWS)
        here = gathered.at[e, :, rows, :]
        pltpu.make_async_remote_copy(
            here, here, first_send.at[e, d], first_recv.at[e, d],
            device_id={"coil": lax.rem(me + 1 + d, COIL)}, device_id_type=MESH,
        ).wait_recv()

    def start_block(k):
        return my_y * WIDE + lax.rem(me, LOW) * FRAME + k

    def start_remote(k):
        return pltpu.make_async_remote_copy(
            image_ref.at[:, :, pl.ds(k * PART, PART), :], primal.at[frame],
            start_send.at[k], start_recv.at[frame],
            device_id=place(*holder(start_block(k))), device_id_type=MESH,
        )

    def start_local(k):
        return pltpu.make_async_copy(
            image_ref.at[:, :, pl.ds(k * PART, PART), :], primal.at[frame], start_send.at[k]
        )

    def ag_copy(e, d):
        return pltpu.make_async_remote_copy(
            rounded.at[e, lax.div(there[d][1], LOW)], gathered.at[e, :, my_block, :],
            ag_send.at[e, d], ag_recv.at[e, d],
            device_id=place(*there[d]), device_id_type=MESH,
        )

    def ag_wait(e, d):
        rows = pl.ds(pl.multiple_of(block_of(*origin[d]) * PART, PART), PART)
        here = gathered.at[e, :, rows, :]
        pltpu.make_async_remote_copy(
            here, here, ag_send.at[e, d], ag_recv.at[e, d],
            device_id=place(*there[d]), device_id_type=MESH,
        ).wait_recv()

    def rs_copy(e, d):
        return pltpu.make_async_remote_copy(
            coded.at[e, block_of(*there[d])], arrived.at[e, my_place],
            rs_send.at[e, d], rs_recv.at[e, d],
            device_id=place(*there[d]), device_id_type=MESH,
        )

    def unit_copy(e, d):
        return pltpu.make_async_remote_copy(
            unit.at[e], units.at[e, my_place], unit_send.at[e, d], unit_recv.at[e, d],
            device_id=place(*there[d]), device_id_type=MESH,
        )

    def halo_copies(e, parity):
        plan = [
            (edges.at[e, 0], halo_rows.at[parity, e, 0], below),
            (edges.at[e, 1], halo_rows.at[parity, e, 1], above),
            (bar.at[e], halo_wide.at[parity, e, 0], behind),
            (bar.at[e], halo_wide.at[parity, e, 1], before),
        ]
        return [
            pltpu.make_async_remote_copy(
                src, dst, halo_send.at[e, i], halo_recv.at[parity, e, i],
                device_id=to, device_id_type=MESH,
            )
            for i, (src, dst, to) in enumerate(plan)
        ]

    my_turn = turned(my_y, my_x)
    my_half = lax.rem(my_turn, FRAME)

    def owner(f):
        return my_y, f * LOW + lax.div(my_turn, FRAME)

    def out_remote(e, f):
        to = place(*owner(f))
        return [
            pltpu.make_async_remote_copy(
                src, dst, out_send.at[e, f, i], out_recv.at[e, my_half, i],
                device_id=to, device_id_type=MESH,
            )
            for i, (src, dst) in enumerate(
                [(last.at[e, f], coded_out.at[e, my_half]), (last_unit.at[e], unit_out.at[e, my_half])]
            )
        ]

    def out_local(e, f):
        return [
            pltpu.make_async_copy(last.at[e, f], coded_out.at[e, my_half], out_send.at[e, f, 0]),
            pltpu.make_async_copy(last_unit.at[e], unit_out.at[e, my_half], out_send.at[e, f, 1]),
        ]

    def out_arrival(e, half):
        return [
            pltpu.make_async_remote_copy(
                dst, dst, out_send.at[e, 0, i], out_recv.at[e, half, i],
                device_id=before, device_id_type=MESH,
            )
            for i, dst in enumerate([coded_out.at[e, half], unit_out.at[e, half]])
        ]

    for e in range(ENC):
        for p in range(2):
            image_load(e, p).wait()
            gathered[e, p, my_rows, :] = image_ref[e, p].astype(BF16)
        for d in range(COIL - 1):
            first_copy(e, d).start()
    for k in range(FRAME):
        y, x = holder(start_block(k))

        @pl.when(x != my_x)
        def _():
            start_remote(k).start()

        @pl.when(x == my_x)
        def _():
            start_local(k).start()

    row_id = lax.broadcasted_iota(jnp.int32, (256, 256), 0)
    col_id = lax.broadcasted_iota(jnp.int32, (256, 256), 1)
    source = jnp.where(row_id < 128, 2 * row_id, 2 * row_id - 255)
    sort_rows = jnp.where(col_id == source, 1.0, 0.0).astype(BF16)

    def sorted_pair(block):
        return jnp.dot(
            sort_rows, block.reshape(256, NCOL), preferred_element_type=F32
        ).astype(BF16)

    loads[0].wait()
    for p in range(2):
        def maps_part(i, carry):
            rows = pl.ds(pl.multiple_of(i * 128, 128), 128)
            both = sorted_pair(maps_raw[p, rows])
            maps_ref[p, 0, rows, :] = both[:128]
            maps_ref[p, 1, rows, :] = both[128:]
            return carry

        lax.fori_loop(0, NR // 128, maps_part, 0)
    loads[2].wait()
    for p in range(2):
        def kspace_part(i, carry):
            e, part = lax.rem(i, ENC), lax.div(i, ENC)
            rows = pl.ds(pl.multiple_of(part * 128, 128), 128)
            both = sorted_pair(kspace_raw[p, rows, e])
            kspace_ref[e, p, 0, rows, :] = both[:128]
            kspace_ref[e, p, 1, rows, :] = both[128:]
            return carry

        lax.fori_loop(0, ENC * NR // 128, kspace_part, 0)
    loads[3].wait()
    loads[4].wait()

    def mask_part(i, carry):
        e, part = lax.rem(i, ENC), lax.div(i, ENC)
        rows = pl.ds(pl.multiple_of(part * 64, 64), 64)
        sampled = mask_ref[e].astype(F32)
        for p in range(2):
            columns = pl.ds(p * NR, NR)
            masked_ref[e, rows, columns] = (
                adjoint_ref[rows, columns].astype(F32) * sampled
            ).astype(BF16)
        return carry

    lax.fori_loop(0, ENC * 2 * NR // 64, mask_part, 0)
    dual[...] = jnp.zeros_like(dual)
    rim_rows[...] = jnp.zeros_like(rim_rows)
    rim_slices[...] = jnp.zeros_like(rim_slices)
    edges[...] = jnp.zeros_like(edges)
    loads[1].wait()
    for k in range(FRAME):
        y, x = holder(start_block(k))

        @pl.when(x != my_x)
        def _():
            start_remote(k).wait_send()

        @pl.when(x == my_x)
        def _():
            start_local(k).wait()

    for f in range(FRAME):
        @pl.when(owner(f)[1] != my_x)
        def _():
            pltpu.make_async_remote_copy(
                primal.at[f], primal.at[f], start_send.at[0], start_recv.at[f],
                device_id=before, device_id_type=MESH,
            ).wait_recv()

    def data_stage(e, outer):
        @pl.when(outer == 0)
        def _():
            for d in range(COIL - 1):
                first_wait(e, d)

        @pl.when(outer != 0)
        def _():
            for d in range(PEERS):
                ag_wait(e, d)

        for c in range(NC):
            map_real, map_imag = maps_ref[0, c].astype(F32), maps_ref[1, c].astype(F32)
            image_real, image_imag = gathered[e, 0].astype(F32), gathered[e, 1].astype(F32)
            coil_data[c, :NR] = (map_real * image_real - map_imag * image_imag).astype(BF16)
            coil_data[c, NR:] = (map_real * image_imag + map_imag * image_real).astype(BF16)
            for p in range(2):
                spectrum = jnp.dot(
                    forward_ref[p * NR : (p + 1) * NR], coil_data[c], preferred_element_type=F32
                )
                residual[c, p * NR : (p + 1) * NR] = (
                    spectrum - kspace_ref[e, p, c].astype(F32)
                ).astype(BF16)
        for c in range(NC):
            map_real, map_imag = maps_ref[0, c].astype(F32), maps_ref[1, c].astype(F32)
            back_real = jnp.dot(masked_ref[e, :NR], residual[c], preferred_element_type=F32)
            back_imag = jnp.dot(masked_ref[e, NR:], residual[c], preferred_element_type=F32)
            grad_real = (map_real * back_real + map_imag * back_imag).reshape(BLOCKS, PART, NCOL)
            grad_imag = (map_real * back_imag - map_imag * back_real).reshape(BLOCKS, PART, NCOL)
            if c == 0:
                partial[:, 0], partial[:, 1] = grad_real, grad_imag
            else:
                partial[:, 0] += grad_real
                partial[:, 1] += grad_imag
        top = jnp.max(jnp.abs(partial[...]), axis=(0, 1, 2), keepdims=True)[0, 0]
        step = jnp.maximum(top, 1e-30) * (1.0 / CODES)
        unit[e] = step
        coded[e] = coded_as(partial[...], 1.0 / step)
        for d in range(PEERS):
            unit_copy(e, d).start()
            rs_copy(e, d).start()
        units[e, my_place] = step
        arrived[e, my_place] = coded[e, mine]

        @pl.when(outer == 0)
        def _():
            for d in range(COIL - 1):
                first_copy(e, d).wait_send()

        @pl.when(outer != 0)
        def _():
            for d in range(PEERS):
                ag_copy(e, d).wait_send()

    def publish(e, x, parity):
        for f in range(FRAME):
            for p in range(2):
                bar[e, f, p] = x[f][p]
                i = 2 * f + p
                edges[e, 0, i : i + 1, :] = x[f][p][PART - 1 : PART]
                edges[e, 1, i : i + 1, :] = x[f][p][0:1]
        for copy in halo_copies(e, parity):
            copy.start()

    def anchor_stage(e, outer):
        for d in range(PEERS):
            unit_copy(e, d).wait_recv()
            rs_copy(e, d).wait_recv()
        x = [[None, None], [None, None]]
        for f in range(FRAME):
            for p in range(2):
                total = jnp.zeros((PART, NCOL), F32)
                for c in range(f * COIL, f * COIL + COIL):
                    total = total + arrived[e, c, p].astype(F32) * units[e, c]
                x[f][p] = primal[f, e, p] - DATA_STEP * total
                anchor[e, f, p] = x[f][p]
                primal[f, e, p] = x[f][p]
        publish(e, x, lax.rem(outer * TV_ITERS, 2))
        for d in range(PEERS):
            unit_copy(e, d).wait_send()
            rs_copy(e, d).wait_send()

    rows_at = lax.broadcasted_iota(jnp.int32, (PART, NCOL), 0)
    cols_at = lax.broadcasted_iota(jnp.int32, (PART, NCOL), 1)
    last_row = rows_at == PART - 1
    first_row = rows_at == 0
    row_keep = jnp.where(jnp.logical_and(last_row, mine == BLOCKS - 1), 0.0, DUAL_STEP)
    rim_keep = jnp.where(mine == 0, 0.0, 1.0)
    slice_keep = jnp.where(cut == CUTS - 1, 0.0, DUAL_STEP)
    rim_slice_keep = jnp.where(cut == 0, 0.0, 1.0)
    col_keep = jnp.where(cols_at == NCOL - 1, 0.0, DUAL_STEP)
    col_back = jnp.where(cols_at == 0, 0.0, 1.0)

    def tv_stage(e, it, outer):
        parity = lax.rem(outer * TV_ITERS + it, 2)
        for copy in halo_copies(e, parity):
            copy.wait_recv()
        for copy in halo_copies(e, parity):
            copy.wait_send()
        both = [[bar[e, f, p] for p in range(2)] for f in range(FRAME)]
        swing = project(*[
            dual[e, 3, 0, p] + DUAL_STEP * (both[1][p] - both[0][p]) for p in range(2)
        ])
        fresh = [[None, None], [None, None]]
        for p in range(2):
            dual[e, 3, 0, p] = swing[p]
            dual[e, 3, 1, p] = -swing[p]
        for f in range(FRAME):
            x = both[f]

            def stepped(k, diffs):
                new = project(*[dual[e, k, f, p] + diffs[p] for p in range(2)])
                for p in range(2):
                    dual[e, k, f, p] = new[p]
                return new

            after = [halo_rows[parity, e, 1, 2 * f + p : 2 * f + p + 1, :] for p in range(2)]
            prior = [halo_rows[parity, e, 0, 2 * f + p : 2 * f + p + 1, :] for p in range(2)]
            rows = stepped(0, [
                row_keep * (jnp.where(last_row, after[p], pltpu.roll(x[p], PART - 1, 0)) - x[p])
                for p in range(2)
            ])
            rim = project(*[
                rim_rows[e, f, p] + DUAL_STEP * (x[p][0:8] - prior[p]) for p in range(2)
            ])
            spread = [None, None]
            for p in range(2):
                edge = rim[p] * rim_keep
                rim_rows[e, f, p] = edge
                spread[p] = rows[p] - jnp.where(first_row, edge[0:1], pltpu.roll(rows[p], 1, 0))
            cols = stepped(1, [col_keep * (pltpu.roll(x[p], NCOL - 1, 1) - x[p]) for p in range(2)])
            for p in range(2):
                spread[p] = spread[p] + (cols[p] - col_back * pltpu.roll(cols[p], 1, 1))
            cuts = stepped(2, [slice_keep * (halo_wide[parity, e, 1, f, p] - x[p]) for p in range(2)])
            rim = project(*[
                rim_slices[e, f, p] + DUAL_STEP * (x[p] - halo_wide[parity, e, 0, f, p])
                for p in range(2)
            ])
            for p in range(2):
                edge = rim[p] * rim_slice_keep
                rim_slices[e, f, p] = edge
                spread[p] = spread[p] + (cuts[p] - edge)
            for p in range(2):
                spread[p] = spread[p] + (2.0 - 4.0 * f) * swing[p]
                held = primal[f, e, p]
                updated = (held + PRIMAL_STEP * spread[p] + PRIMAL_STEP * anchor[e, f, p]) * (
                    1.0 / (1.0 + PRIMAL_STEP)
                )
                primal[f, e, p] = updated
                fresh[f][p] = 2.0 * updated - held

        @pl.when(it < TV_ITERS - 1)
        def _():
            publish(e, fresh, 1 - parity)

        @pl.when(jnp.logical_and(it == TV_ITERS - 1, outer < OUTER - 1))
        def _():
            for f in range(FRAME):
                for p in range(2):
                    rounded[e, f, p] = primal[f, e, p].astype(BF16)
            for d in range(PEERS):
                ag_copy(e, d).start()
            for p in range(2):
                gathered[e, p, my_block, :] = rounded[e, frame, p]

        @pl.when(jnp.logical_and(it == TV_ITERS - 1, outer == OUTER - 1))
        def _():
            top = jnp.max(jnp.abs(primal[:, e]), axis=(0, 1, 2), keepdims=True)[0, 0]
            step = jnp.maximum(top, 1e-30) * (1.0 / CODES)
            last_unit[e] = step
            for f in range(FRAME):
                last[e, f, 4] = coded_as(primal[f, e], 1.0 / step)
                for k in range(4):
                    last[e, f, k] = coded_as(dual[e, k, f], CODES / SMOOTH_WEIGHT)
            for f in range(FRAME):
                @pl.when(owner(f)[1] != my_x)
                def _():
                    for copy in out_remote(e, f):
                        copy.start()

                @pl.when(owner(f)[1] == my_x)
                def _():
                    for copy in out_local(e, f):
                        copy.start()

    def slot(t, carry):
        def one(i, carry):
            e = ENC - 1 - i
            at = t - e
            outer = lax.div(at, STAGES)
            stage = lax.rem(at, STAGES)
            active = jnp.logical_and(at >= 0, at < OUTER * STAGES)

            @pl.when(jnp.logical_and(active, stage == 0))
            def _():
                data_stage(e, outer)

            @pl.when(jnp.logical_and(active, stage == 2))
            def _():
                anchor_stage(e, outer)

            @pl.when(jnp.logical_and(active, jnp.logical_and(stage >= 3, stage < 3 + TV_ITERS)))
            def _():
                tv_stage(e, stage - 3, outer)

            return carry

        return lax.fori_loop(0, ENC, one, carry)

    lax.fori_loop(0, OUTER * STAGES + ENC - 1, slot, 0)

    def finish(e, carry):
        for f in range(FRAME):
            @pl.when(owner(f)[1] != my_x)
            def _():
                for copy in out_remote(e, f):
                    copy.wait_send()

            @pl.when(owner(f)[1] == my_x)
            def _():
                for copy in out_local(e, f):
                    copy.wait()

        for half in range(FRAME):
            @pl.when(holder(start_block(half))[1] != my_x)
            def _():
                for copy in out_arrival(e, half):
                    copy.wait_recv()

        return carry

    lax.fori_loop(0, ENC, finish, 0)


def restore(coded_hbm, unit_hbm, image_out, dual_out, coded, unit, values, load_sem, out_sem):
    ENC, FRAME, KINDS, _, PART, NCOL = coded.shape
    loads = [pltpu.make_async_copy(unit_hbm, unit, load_sem.at[ENC])]
    loads += [
        pltpu.make_async_copy(coded_hbm.at[e], coded.at[e], load_sem.at[e]) for e in range(ENC)
    ]
    for load in loads:
        load.start()
    loads[0].wait()

    def stores(e):
        copies = []
        for p in range(2):
            for k in range(KINDS):
                if k == KINDS - 1:
                    to = image_out.at[:, p * ENC + e, 0, :]
                else:
                    to = dual_out.at[k, :, p * ENC + e, 0, :]
                copies.append(
                    pltpu.make_async_copy(values.at[e, k, p], to, out_sem.at[e, k, p])
                )
        return copies

    for e in range(ENC):
        loads[1 + e].wait()
        for half in range(FRAME):
            rows = pl.ds(half * PART, PART)
            for p in range(2):
                for k in range(KINDS):
                    step = unit[e, half] if k == KINDS - 1 else SMOOTH_WEIGHT / CODES
                    values[e, k, p, rows, :] = coded[e, half, k, p].astype(F32) * step
        for copy in stores(e):
            copy.start()
    for e in range(ENC):
        for copy in stores(e):
            copy.wait()


def solution(mesh):
    COIL, CUTS, FRAME = mesh.shape["coil"], mesh.shape["cuts"], mesh.shape["frame"]

    def shards(kspace, coil_maps, sampling_masks, start_image):
        _, NR, ENC, _, _, NC, NCOL = kspace.shape
        ROWS = start_image.shape[0]
        PART = ROWS // FRAME
        peers = FRAME * COIL - 1
        forward_table, adjoint_table = transform_tables(NR)
        hbm = pl.BlockSpec(memory_space=pltpu.HBM)
        dma = pltpu.SemaphoreType.DMA
        coded, unit = pl.pallas_call(
            functools.partial(kernel, (NR, NCOL, NC, ENC, COIL, CUTS, FRAME)),
            out_shape=(
                jax.ShapeDtypeStruct((ENC, FRAME, 5, 2, PART, NCOL), I16),
                jax.ShapeDtypeStruct((ENC, FRAME, 1, NCOL), F32),
            ),
            in_specs=[hbm] * 6,
            out_specs=(hbm, hbm),
            scratch_shapes=[
                pltpu.VMEM((2, NR, ENC, NC, NCOL), BF16),
                pltpu.VMEM((2, NR, NC, NCOL), BF16),
                pltpu.VMEM((ENC, 2, NC, NR, NCOL), BF16),
                pltpu.VMEM((2, NC, NR, NCOL), BF16),
                pltpu.VMEM((2 * NR, 2 * NR), BF16),
                pltpu.VMEM((2 * NR, 2 * NR), BF16),
                pltpu.VMEM((ENC, 2 * NR, 2 * NR), BF16),
                pltpu.VMEM((ENC, 1, NR), jnp.int32),
                pltpu.VMEM((ENC, 2, ROWS, NCOL), F32),
                pltpu.VMEM((ENC, FRAME, 2, PART, NCOL), BF16),
                pltpu.VMEM((ENC, 2, NR, NCOL), BF16),
                pltpu.VMEM((NC, 2 * NR, NCOL), BF16),
                pltpu.VMEM((NC, 2 * NR, NCOL), BF16),
                pltpu.VMEM((NR // PART, 2, PART, NCOL), F32),
                pltpu.VMEM((ENC, NR // PART, 2, PART, NCOL), I16),
                pltpu.VMEM((ENC, 1, NCOL), F32),
                pltpu.VMEM((ENC, FRAME * COIL, 2, PART, NCOL), I16),
                pltpu.VMEM((ENC, FRAME * COIL, 1, NCOL), F32),
                pltpu.VMEM((FRAME, ENC, 2, PART, NCOL), F32),
                pltpu.VMEM((ENC, FRAME, 2, PART, NCOL), F32),
                pltpu.VMEM((ENC, FRAME, 2, PART, NCOL), F32),
                pltpu.VMEM((ENC, 4, FRAME, 2, PART, NCOL), F32),
                pltpu.VMEM((ENC, FRAME, 2, 8, NCOL), F32),
                pltpu.VMEM((ENC, FRAME, 2, PART, NCOL), F32),
                pltpu.VMEM((ENC, 2, 8, NCOL), F32),
                pltpu.VMEM((2, ENC, 2, 8, NCOL), F32),
                pltpu.VMEM((2, ENC, 2, FRAME, 2, PART, NCOL), F32),
                pltpu.VMEM((ENC, FRAME, 5, 2, PART, NCOL), I16),
                pltpu.VMEM((ENC, 1, NCOL), F32),
                dma((2 * ENC + 5,)),
                dma((ENC, COIL - 1)),
                dma((ENC, COIL - 1)),
                dma((FRAME,)),
                dma((FRAME,)),
                dma((ENC, peers)),
                dma((ENC, peers)),
                dma((ENC, peers)),
                dma((ENC, peers)),
                dma((ENC, peers)),
                dma((ENC, peers)),
                dma((ENC, 4)),
                dma((2, ENC, 4)),
                dma((ENC, FRAME, 2)),
                dma((ENC, FRAME, 2)),
            ],
            compiler_params=pltpu.CompilerParams(
                collective_id=0, has_side_effects=True, vmem_limit_bytes=60 << 20
            ),
            name="sense_tv",
        )(
            kspace.reshape(2, NR, ENC, NC, NCOL),
            coil_maps.reshape(2, NR, NC, NCOL),
            sampling_masks.reshape(ENC, 1, NR),
            start_image.reshape(ROWS, 2 * ENC, 1, NCOL),
            jnp.asarray(forward_table),
            jnp.asarray(adjoint_table),
        )
        image, dual = pl.pallas_call(
            restore,
            out_shape=(
                jax.ShapeDtypeStruct((ROWS, 2 * ENC, 1, NCOL), F32),
                jax.ShapeDtypeStruct((4, ROWS, 2 * ENC, 1, NCOL), F32),
            ),
            in_specs=[hbm, hbm],
            out_specs=(hbm, hbm),
            scratch_shapes=[
                pltpu.VMEM((ENC, FRAME, 5, 2, PART, NCOL), I16),
                pltpu.VMEM((ENC, FRAME, 1, NCOL), F32),
                pltpu.VMEM((ENC, 5, 2, ROWS, NCOL), F32),
                dma((ENC + 1,)),
                dma((ENC, 5, 2)),
            ],
            compiler_params=pltpu.CompilerParams(vmem_limit_bytes=60 << 20),
            name="restore",
        )(coded, unit)
        return (
            image.reshape(ROWS, 2, ENC, 1, 1, NCOL),
            dual.reshape(4, ROWS, 2, ENC, 1, 1, NCOL),
        )

    return jax.shard_map(
        shards,
        mesh=mesh,
        in_specs=(
            P(None, None, None, "frame", "cuts", "coil", None),
            P(None, None, "cuts", "coil", None),
            P("frame", None, None),
            P("coil", None, None, "frame", "cuts", None),
        ),
        out_specs=(
            P("coil", None, None, "frame", "cuts", None),
            P(None, "coil", None, None, "frame", "cuts", None),
        ),
        check_vma=False,
    )
```

```python
import functools

import jax
import jax.numpy as jnp
import ml_dtypes
import numpy as np
from jax import lax
from jax.experimental import pallas as pl
from jax.experimental.pallas import tpu as pltpu
from jax.sharding import PartitionSpec as P

OUTER = 2
TV_ITERS = 3
STAGES = TV_ITERS + 4

DATA_STEP = 0.5
DUAL_STEP = 0.25
PRIMAL_STEP = 0.25
SMOOTH_WEIGHT = 0.3

MESH = pl.DeviceIdType.MESH
BF16 = jnp.bfloat16
F32 = jnp.float32
I16 = jnp.int16
CODES = 32000.0


def transform_tables(length):
    position = np.arange(length, dtype=np.int64)
    phase_grid = (position[:, None] * position[None, :]) % length
    angles = phase_grid.astype(np.float32) * np.float32(2.0 * np.pi / length)
    norming = np.float32(1.0) / np.sqrt(np.float32(length))
    real_part = (np.cos(angles) * norming).astype(ml_dtypes.bfloat16)
    imag_part = (-np.sin(angles) * norming).astype(ml_dtypes.bfloat16)
    forward_table = np.block([[real_part, -imag_part], [imag_part, real_part]])
    adjoint_table = np.block([[real_part, imag_part], [-imag_part, real_part]])
    return forward_table, adjoint_table


def coded_as(values, per_unit):
    return jnp.round(values * per_unit).astype(jnp.int32).astype(I16)


def project(real_part, imag_part):
    factor = jnp.minimum(
        SMOOTH_WEIGHT * lax.rsqrt(real_part * real_part + imag_part * imag_part), 1.0
    )
    return real_part * factor, imag_part * factor


def kernel(
    sizes,
    kspace_hbm, maps_hbm, mask_hbm, image_hbm, forward_hbm, adjoint_hbm,
    coded_out, unit_out,
    kspace_raw, maps_raw, kspace_ref, maps_ref, forward_ref, adjoint_ref, masked_ref,
    mask_ref, image_ref, rounded, gathered, coil_data, residual, partial, coded, unit, arrived, units,
    primal, anchor, bar, dual, rim_rows, rim_slices, edges, halo_rows, halo_wide,
    last, last_unit,
    load_sem, first_send, first_recv, start_send, start_recv, ag_send, ag_recv,
    rs_send, rs_recv, unit_send, unit_recv, halo_send, halo_recv, out_send, out_recv,
):
    NR, NCOL, NC, ENC, COIL, CUTS, FRAME = sizes
    ROWS = NR // COIL
    PART = ROWS // FRAME
    LOW = COIL // 4
    WIDE = LOW * FRAME
    BLOCKS = 4 * WIDE
    me = lax.axis_index("coil")
    cut = lax.axis_index("cuts")
    frame = lax.axis_index("frame")
    my_y, my_x = lax.div(me, LOW), frame * LOW + lax.rem(me, LOW)

    def place(y, x):
        return {"coil": y * LOW + lax.rem(x, LOW), "frame": lax.div(x, LOW)}

    def turned(y, x):
        return jnp.where(lax.rem(y, 2) == 0, x, WIDE - 1 - x)

    def block_of(y, x):
        return y * WIDE + turned(y, x)

    def holder(block):
        y = lax.div(block, WIDE)
        return y, turned(y, lax.rem(block, WIDE))

    mine = block_of(my_y, my_x)
    my_block = pl.ds(pl.multiple_of(mine * PART, PART), PART)
    my_rows = pl.ds(pl.multiple_of(me * ROWS, ROWS), ROWS)
    my_place = frame * COIL + me

    offsets = [(dy, dx) for dy in range(4) for dx in range(WIDE) if (dy, dx) != (0, 0)]
    PEERS = len(offsets)
    there = [(lax.rem(my_y + dy, 4), lax.rem(my_x + dx, WIDE)) for dy, dx in offsets]
    above = place(*holder(lax.rem(mine + BLOCKS - 1, BLOCKS)))
    below = place(*holder(lax.rem(mine + 1, BLOCKS)))
    before, behind = {"cuts": lax.rem(cut + CUTS - 1, CUTS)}, {"cuts": lax.rem(cut + 1, CUTS)}

    barrier = pltpu.get_barrier_semaphore()
    greeted = [place(*t) for t in there[::-1]] + [before, behind]
    for other in greeted:
        pl.semaphore_signal(barrier, inc=1, device_id=other, device_id_type=MESH)

    def image_load(e, p):
        return pltpu.make_async_copy(
            image_hbm.at[:, p * ENC + e, 0, :], image_ref.at[e, p], load_sem.at[2 * e + p]
        )

    def plain_load(src, dst, i):
        return pltpu.make_async_copy(src, dst, load_sem.at[2 * ENC + i])

    loads = [
        plain_load(maps_hbm, maps_raw, 0),
        plain_load(forward_hbm, forward_ref, 1),
        plain_load(kspace_hbm, kspace_raw, 2),
        plain_load(adjoint_hbm, adjoint_ref, 3),
        plain_load(mask_hbm, mask_ref, 4),
    ]
    for e in range(ENC):
        for p in range(2):
            image_load(e, p).start()
    for load in loads:
        load.start()

    for e in range(ENC):
        for p in range(2):
            image_load(e, p).wait()
            gathered[e, p, my_rows, :] = image_ref[e, p].astype(BF16)
    pl.semaphore_wait(barrier, len(greeted))

    def first_copy(e, d):
        other = {"coil": lax.rem(me + 1 + d, COIL)}
        return pltpu.make_async_remote_copy(
            gathered.at[e, :, my_rows, :], gathered.at[e, :, my_rows, :],
            first_send.at[e], first_recv.at[e], device_id=other, device_id_type=MESH,
        )

    def all_of(part, send, recv):
        return pltpu.make_async_remote_copy(
            part, part, send, recv, device_id=before, device_id_type=MESH
        )

    def first_all(e):
        rows = pl.ds(0, (COIL - 1) * ROWS)
        return all_of(gathered.at[e, :, rows, :], first_send.at[e], first_recv.at[e])

    def ag_all(e):
        rows = pl.ds(0, PEERS * PART)
        return all_of(gathered.at[e, :, rows, :], ag_send.at[e], ag_recv.at[e])

    def rs_all(e):
        return all_of(arrived.at[e, pl.ds(0, PEERS)], rs_send.at[e], rs_recv.at[e])

    def unit_all(e):
        return all_of(units.at[e, pl.ds(0, PEERS)], unit_send.at[e], unit_recv.at[e])

    def start_block(k):
        return my_y * WIDE + lax.rem(me, LOW) * FRAME + k

    def start_remote(k):
        return pltpu.make_async_remote_copy(
            image_ref.at[:, :, pl.ds(k * PART, PART), :], primal.at[frame],
            start_send.at[k], start_recv.at[frame],
            device_id=place(*holder(start_block(k))), device_id_type=MESH,
        )

    def start_local(k):
        return pltpu.make_async_copy(
            image_ref.at[:, :, pl.ds(k * PART, PART), :], primal.at[frame], start_send.at[k]
        )

    def ag_copy(e, d):
        return pltpu.make_async_remote_copy(
            rounded.at[e, lax.div(there[d][1], LOW)], gathered.at[e, :, my_block, :],
            ag_send.at[e], ag_recv.at[e],
            device_id=place(*there[d]), device_id_type=MESH,
        )

    def rs_copy(e, d):
        return pltpu.make_async_remote_copy(
            coded.at[e, block_of(*there[d])], arrived.at[e, my_place],
            rs_send.at[e], rs_recv.at[e],
            device_id=place(*there[d]), device_id_type=MESH,
        )

    def unit_copy(e, d):
        return pltpu.make_async_remote_copy(
            unit.at[e], units.at[e, my_place], unit_send.at[e], unit_recv.at[e],
            device_id=place(*there[d]), device_id_type=MESH,
        )

    def halo_copies(e, parity):
        plan = [
            (edges.at[e, 0], halo_rows.at[parity, e, 0], below),
            (edges.at[e, 1], halo_rows.at[parity, e, 1], above),
            (bar.at[e], halo_wide.at[parity, e, 0], behind),
            (bar.at[e], halo_wide.at[parity, e, 1], before),
        ]
        return [
            pltpu.make_async_remote_copy(
                src, dst, halo_send.at[e, i], halo_recv.at[parity, e, i],
                device_id=to, device_id_type=MESH,
            )
            for i, (src, dst, to) in enumerate(plan)
        ]

    my_turn = turned(my_y, my_x)
    my_half = lax.rem(my_turn, FRAME)

    def owner(f):
        return my_y, f * LOW + lax.div(my_turn, FRAME)

    def out_remote(e, f):
        to = place(*owner(f))
        return [
            pltpu.make_async_remote_copy(
                src, dst, out_send.at[e, f, i], out_recv.at[e, my_half, i],
                device_id=to, device_id_type=MESH,
            )
            for i, (src, dst) in enumerate(
                [(last.at[e, f], coded_out.at[e, my_half]), (last_unit.at[e], unit_out.at[e, my_half])]
            )
        ]

    def out_local(e, f):
        return [
            pltpu.make_async_copy(last.at[e, f], coded_out.at[e, my_half], out_send.at[e, f, 0]),
            pltpu.make_async_copy(last_unit.at[e], unit_out.at[e, my_half], out_send.at[e, f, 1]),
        ]

    def out_arrival(e, half):
        return [
            pltpu.make_async_remote_copy(
                dst, dst, out_send.at[e, 0, i], out_recv.at[e, half, i],
                device_id=before, device_id_type=MESH,
            )
            for i, dst in enumerate([coded_out.at[e, half], unit_out.at[e, half]])
        ]

    for e in range(ENC):
        for d in range(COIL - 1):
            first_copy(e, d).start()
    for k in range(FRAME):
        y, x = holder(start_block(k))

        @pl.when(x != my_x)
        def _():
            start_remote(k).start()

        @pl.when(x == my_x)
        def _():
            start_local(k).start()

    row_id = lax.broadcasted_iota(jnp.int32, (256, 256), 0)
    col_id = lax.broadcasted_iota(jnp.int32, (256, 256), 1)
    source = jnp.where(row_id < 128, 2 * row_id, 2 * row_id - 255)
    sort_rows = jnp.where(col_id == source, 1.0, 0.0).astype(BF16)

    def sorted_pair(block):
        return jnp.dot(
            sort_rows, block.reshape(256, NCOL), preferred_element_type=F32
        ).astype(BF16)

    loads[0].wait()
    for p in range(2):
        def maps_part(i, carry):
            rows = pl.ds(pl.multiple_of(i * 128, 128), 128)
            both = sorted_pair(maps_raw[p, rows])
            maps_ref[p, 0, rows, :] = both[:128]
            maps_ref[p, 1, rows, :] = both[128:]
            return carry

        lax.fori_loop(0, NR // 128, maps_part, 0)
    loads[2].wait()
    for p in range(2):
        def kspace_part(i, carry):
            e, part = lax.rem(i, ENC), lax.div(i, ENC)
            rows = pl.ds(pl.multiple_of(part * 128, 128), 128)
            both = sorted_pair(kspace_raw[p, rows, e])
            kspace_ref[e, p, 0, rows, :] = both[:128]
            kspace_ref[e, p, 1, rows, :] = both[128:]
            return carry

        lax.fori_loop(0, ENC * NR // 128, kspace_part, 0)
    loads[3].wait()
    loads[4].wait()

    def mask_part(i, carry):
        e, part = lax.rem(i, ENC), lax.div(i, ENC)
        rows = pl.ds(pl.multiple_of(part * 64, 64), 64)
        sampled = mask_ref[e].astype(F32)
        for p in range(2):
            columns = pl.ds(p * NR, NR)
            masked_ref[e, rows, columns] = (
                adjoint_ref[rows, columns].astype(F32) * sampled
            ).astype(BF16)
        return carry

    lax.fori_loop(0, ENC * 2 * NR // 64, mask_part, 0)
    dual[...] = jnp.zeros_like(dual)
    rim_rows[...] = jnp.zeros_like(rim_rows)
    rim_slices[...] = jnp.zeros_like(rim_slices)
    edges[...] = jnp.zeros_like(edges)
    loads[1].wait()
    def data_stage(e, outer):
        @pl.when(outer == 0)
        def _():
            first_all(e).wait_recv()

        @pl.when(outer != 0)
        def _():
            ag_all(e).wait_recv()

        for c in range(NC):
            map_real, map_imag = maps_ref[0, c].astype(F32), maps_ref[1, c].astype(F32)
            image_real, image_imag = gathered[e, 0].astype(F32), gathered[e, 1].astype(F32)
            coil_data[c, :NR] = (map_real * image_real - map_imag * image_imag).astype(BF16)
            coil_data[c, NR:] = (map_real * image_imag + map_imag * image_real).astype(BF16)
            for p in range(2):
                spectrum = jnp.dot(
                    forward_ref[p * NR : (p + 1) * NR], coil_data[c], preferred_element_type=F32
                )
                residual[c, p * NR : (p + 1) * NR] = (
                    spectrum - kspace_ref[e, p, c].astype(F32)
                ).astype(BF16)
        for c in range(NC):
            map_real, map_imag = maps_ref[0, c].astype(F32), maps_ref[1, c].astype(F32)
            back_real = jnp.dot(masked_ref[e, :NR], residual[c], preferred_element_type=F32)
            back_imag = jnp.dot(masked_ref[e, NR:], residual[c], preferred_element_type=F32)
            grad_real = (map_real * back_real + map_imag * back_imag).reshape(BLOCKS, PART, NCOL)
            grad_imag = (map_real * back_imag - map_imag * back_real).reshape(BLOCKS, PART, NCOL)
            if c == 0:
                partial[:, 0], partial[:, 1] = grad_real, grad_imag
            else:
                partial[:, 0] += grad_real
                partial[:, 1] += grad_imag
        top = jnp.max(jnp.abs(partial[...]), axis=(0, 1, 2), keepdims=True)[0, 0]
        step = jnp.maximum(top, 1e-30) * (1.0 / CODES)
        unit[e] = step
        coded[e] = coded_as(partial[...], 1.0 / step)
        for d in range(PEERS):
            unit_copy(e, d).start()
            rs_copy(e, d).start()
        units[e, my_place] = step
        arrived[e, my_place] = coded[e, mine]

        @pl.when(outer == 0)
        def _():
            first_all(e).wait_send()

        @pl.when(outer != 0)
        def _():
            ag_all(e).wait_send()

    def publish(e, x, parity):
        for f in range(FRAME):
            for p in range(2):
                bar[e, f, p] = x[f][p]
                i = 2 * f + p
                edges[e, 0, i : i + 1, :] = x[f][p][PART - 1 : PART]
                edges[e, 1, i : i + 1, :] = x[f][p][0:1]
        for copy in halo_copies(e, parity):
            copy.start()

    def start_wait():
        for k in range(FRAME):
            y, x = holder(start_block(k))

            @pl.when(x != my_x)
            def _():
                start_remote(k).wait_send()

            @pl.when(x == my_x)
            def _():
                start_local(k).wait()

        for f in range(FRAME):
            @pl.when(owner(f)[1] != my_x)
            def _():
                pltpu.make_async_remote_copy(
                    primal.at[f], primal.at[f], start_send.at[0], start_recv.at[f],
                    device_id=before, device_id_type=MESH,
                ).wait_recv()

    def anchor_stage(e, outer):
        pl.when(jnp.logical_and(e == 0, outer == 0))(start_wait)
        unit_all(e).wait_recv()
        rs_all(e).wait_recv()
        x = [[None, None], [None, None]]
        for f in range(FRAME):
            for p in range(2):
                total = jnp.zeros((PART, NCOL), F32)
                for c in range(f * COIL, f * COIL + COIL):
                    total = total + arrived[e, c, p].astype(F32) * units[e, c]
                x[f][p] = primal[f, e, p] - DATA_STEP * total
                anchor[e, f, p] = x[f][p]
                primal[f, e, p] = x[f][p]
        publish(e, x, lax.rem(outer * TV_ITERS, 2))
        unit_all(e).wait_send()
        rs_all(e).wait_send()

    rows_at = lax.broadcasted_iota(jnp.int32, (PART, NCOL), 0)
    cols_at = lax.broadcasted_iota(jnp.int32, (PART, NCOL), 1)
    last_row = rows_at == PART - 1
    first_row = rows_at == 0
    row_keep = jnp.where(jnp.logical_and(last_row, mine == BLOCKS - 1), 0.0, DUAL_STEP)
    rim_keep = jnp.where(mine == 0, 0.0, 1.0)
    slice_keep = jnp.where(cut == CUTS - 1, 0.0, DUAL_STEP)
    rim_slice_keep = jnp.where(cut == 0, 0.0, 1.0)
    col_keep = jnp.where(cols_at == NCOL - 1, 0.0, DUAL_STEP)
    col_back = jnp.where(cols_at == 0, 0.0, 1.0)

    def tv_stage(e, it, outer):
        parity = lax.rem(outer * TV_ITERS + it, 2)
        for copy in halo_copies(e, parity):
            copy.wait_recv()
        for copy in halo_copies(e, parity):
            copy.wait_send()
        both = [[bar[e, f, p] for p in range(2)] for f in range(FRAME)]
        swing = project(*[
            dual[e, 3, 0, p] + DUAL_STEP * (both[1][p] - both[0][p]) for p in range(2)
        ])
        fresh = [[None, None], [None, None]]
        for p in range(2):
            dual[e, 3, 0, p] = swing[p]
            dual[e, 3, 1, p] = -swing[p]
        for f in range(FRAME):
            x = both[f]

            def stepped(k, diffs):
                new = project(*[dual[e, k, f, p] + diffs[p] for p in range(2)])
                for p in range(2):
                    dual[e, k, f, p] = new[p]
                return new

            after = [halo_rows[parity, e, 1, 2 * f + p : 2 * f + p + 1, :] for p in range(2)]
            prior = [halo_rows[parity, e, 0, 2 * f + p : 2 * f + p + 1, :] for p in range(2)]
            rows = stepped(0, [
                row_keep * (jnp.where(last_row, after[p], pltpu.roll(x[p], PART - 1, 0)) - x[p])
                for p in range(2)
            ])
            rim = project(*[
                rim_rows[e, f, p] + DUAL_STEP * (x[p][0:8] - prior[p]) for p in range(2)
            ])
            spread = [None, None]
            for p in range(2):
                edge = rim[p] * rim_keep
                rim_rows[e, f, p] = edge
                spread[p] = rows[p] - jnp.where(first_row, edge[0:1], pltpu.roll(rows[p], 1, 0))
            cols = stepped(1, [col_keep * (pltpu.roll(x[p], NCOL - 1, 1) - x[p]) for p in range(2)])
            for p in range(2):
                spread[p] = spread[p] + (cols[p] - col_back * pltpu.roll(cols[p], 1, 1))
            cuts = stepped(2, [slice_keep * (halo_wide[parity, e, 1, f, p] - x[p]) for p in range(2)])
            rim = project(*[
                rim_slices[e, f, p] + DUAL_STEP * (x[p] - halo_wide[parity, e, 0, f, p])
                for p in range(2)
            ])
            for p in range(2):
                edge = rim[p] * rim_slice_keep
                rim_slices[e, f, p] = edge
                spread[p] = spread[p] + (cuts[p] - edge)
            for p in range(2):
                spread[p] = spread[p] + (2.0 - 4.0 * f) * swing[p]
                held = primal[f, e, p]
                updated = (held + PRIMAL_STEP * spread[p] + PRIMAL_STEP * anchor[e, f, p]) * (
                    1.0 / (1.0 + PRIMAL_STEP)
                )
                primal[f, e, p] = updated
                fresh[f][p] = 2.0 * updated - held

        @pl.when(it < TV_ITERS - 1)
        def _():
            publish(e, fresh, 1 - parity)

        @pl.when(jnp.logical_and(it == TV_ITERS - 1, outer < OUTER - 1))
        def _():
            for f in range(FRAME):
                for p in range(2):
                    rounded[e, f, p] = primal[f, e, p].astype(BF16)
            for d in range(PEERS):
                ag_copy(e, d).start()
            for p in range(2):
                gathered[e, p, my_block, :] = rounded[e, frame, p]

        @pl.when(jnp.logical_and(it == TV_ITERS - 1, outer == OUTER - 1))
        def _():
            top = jnp.max(jnp.abs(primal[:, e]), axis=(0, 1, 2), keepdims=True)[0, 0]
            step = jnp.maximum(top, 1e-30) * (1.0 / CODES)
            last_unit[e] = step
            for f in range(FRAME):
                last[e, f, 4] = coded_as(primal[f, e], 1.0 / step)
                for k in range(4):
                    last[e, f, k] = coded_as(dual[e, k, f], CODES / SMOOTH_WEIGHT)
            for f in range(FRAME):
                @pl.when(owner(f)[1] != my_x)
                def _():
                    for copy in out_remote(e, f):
                        copy.start()

                @pl.when(owner(f)[1] == my_x)
                def _():
                    for copy in out_local(e, f):
                        copy.start()

    def slot(t, carry):
        def one(i, carry):
            e = ENC - 1 - i
            at = t - e
            outer = lax.div(at, STAGES)
            stage = lax.rem(at, STAGES)
            active = jnp.logical_and(at >= 0, at < OUTER * STAGES)

            @pl.when(jnp.logical_and(active, stage == 0))
            def _():
                data_stage(e, outer)

            @pl.when(jnp.logical_and(active, stage == 2))
            def _():
                anchor_stage(e, outer)

            @pl.when(jnp.logical_and(active, jnp.logical_and(stage >= 3, stage < 3 + TV_ITERS)))
            def _():
                tv_stage(e, stage - 3, outer)

            return carry

        return lax.fori_loop(0, ENC, one, carry)

    lax.fori_loop(0, OUTER * STAGES + ENC - 1, slot, 0)

    def finish(e, carry):
        for f in range(FRAME):
            @pl.when(owner(f)[1] != my_x)
            def _():
                for copy in out_remote(e, f):
                    copy.wait_send()

            @pl.when(owner(f)[1] == my_x)
            def _():
                for copy in out_local(e, f):
                    copy.wait()

        for half in range(FRAME):
            @pl.when(holder(start_block(half))[1] != my_x)
            def _():
                for copy in out_arrival(e, half):
                    copy.wait_recv()

        return carry

    lax.fori_loop(0, ENC, finish, 0)


def restore(coded_hbm, unit_hbm, image_out, dual_out, coded, unit, values, load_sem, out_sem):
    ENC, FRAME, KINDS, _, PART, NCOL = coded.shape
    loads = [pltpu.make_async_copy(unit_hbm, unit, load_sem.at[ENC])]
    loads += [
        pltpu.make_async_copy(coded_hbm.at[e], coded.at[e], load_sem.at[e]) for e in range(ENC)
    ]
    for load in loads:
        load.start()
    loads[0].wait()

    def stores(e):
        copies = []
        for p in range(2):
            for k in range(KINDS):
                if k == KINDS - 1:
                    to = image_out.at[:, p * ENC + e, 0, :]
                else:
                    to = dual_out.at[k, :, p * ENC + e, 0, :]
                copies.append(
                    pltpu.make_async_copy(values.at[e, k, p], to, out_sem.at[e, k, p])
                )
        return copies

    for e in range(ENC):
        loads[1 + e].wait()
        for half in range(FRAME):
            rows = pl.ds(half * PART, PART)
            for p in range(2):
                for k in range(KINDS):
                    step = unit[e, half] if k == KINDS - 1 else SMOOTH_WEIGHT / CODES
                    values[e, k, p, rows, :] = coded[e, half, k, p].astype(F32) * step
        for copy in stores(e):
            copy.start()
    for e in range(ENC):
        for copy in stores(e):
            copy.wait()


def solution(mesh):
    COIL, CUTS, FRAME = mesh.shape["coil"], mesh.shape["cuts"], mesh.shape["frame"]

    def shards(kspace, coil_maps, sampling_masks, start_image):
        _, NR, ENC, _, _, NC, NCOL = kspace.shape
        ROWS = start_image.shape[0]
        PART = ROWS // FRAME
        forward_table, adjoint_table = transform_tables(NR)
        hbm = pl.BlockSpec(memory_space=pltpu.HBM)
        dma = pltpu.SemaphoreType.DMA
        coded, unit = pl.pallas_call(
            functools.partial(kernel, (NR, NCOL, NC, ENC, COIL, CUTS, FRAME)),
            out_shape=(
                jax.ShapeDtypeStruct((ENC, FRAME, 5, 2, PART, NCOL), I16),
                jax.ShapeDtypeStruct((ENC, FRAME, 1, NCOL), F32),
            ),
            in_specs=[hbm] * 6,
            out_specs=(hbm, hbm),
            scratch_shapes=[
                pltpu.VMEM((2, NR, ENC, NC, NCOL), BF16),
                pltpu.VMEM((2, NR, NC, NCOL), BF16),
                pltpu.VMEM((ENC, 2, NC, NR, NCOL), BF16),
                pltpu.VMEM((2, NC, NR, NCOL), BF16),
                pltpu.VMEM((2 * NR, 2 * NR), BF16),
                pltpu.VMEM((2 * NR, 2 * NR), BF16),
                pltpu.VMEM((ENC, 2 * NR, 2 * NR), BF16),
                pltpu.VMEM((ENC, 1, NR), jnp.int32),
                pltpu.VMEM((ENC, 2, ROWS, NCOL), F32),
                pltpu.VMEM((ENC, FRAME, 2, PART, NCOL), BF16),
                pltpu.VMEM((ENC, 2, NR, NCOL), BF16),
                pltpu.VMEM((NC, 2 * NR, NCOL), BF16),
                pltpu.VMEM((NC, 2 * NR, NCOL), BF16),
                pltpu.VMEM((NR // PART, 2, PART, NCOL), F32),
                pltpu.VMEM((ENC, NR // PART, 2, PART, NCOL), I16),
                pltpu.VMEM((ENC, 1, NCOL), F32),
                pltpu.VMEM((ENC, FRAME * COIL, 2, PART, NCOL), I16),
                pltpu.VMEM((ENC, FRAME * COIL, 1, NCOL), F32),
                pltpu.VMEM((FRAME, ENC, 2, PART, NCOL), F32),
                pltpu.VMEM((ENC, FRAME, 2, PART, NCOL), F32),
                pltpu.VMEM((ENC, FRAME, 2, PART, NCOL), F32),
                pltpu.VMEM((ENC, 4, FRAME, 2, PART, NCOL), F32),
                pltpu.VMEM((ENC, FRAME, 2, 8, NCOL), F32),
                pltpu.VMEM((ENC, FRAME, 2, PART, NCOL), F32),
                pltpu.VMEM((ENC, 2, 8, NCOL), F32),
                pltpu.VMEM((2, ENC, 2, 8, NCOL), F32),
                pltpu.VMEM((2, ENC, 2, FRAME, 2, PART, NCOL), F32),
                pltpu.VMEM((ENC, FRAME, 5, 2, PART, NCOL), I16),
                pltpu.VMEM((ENC, 1, NCOL), F32),
                dma((2 * ENC + 5,)),
                dma((ENC,)),
                dma((ENC,)),
                dma((FRAME,)),
                dma((FRAME,)),
                dma((ENC,)),
                dma((ENC,)),
                dma((ENC,)),
                dma((ENC,)),
                dma((ENC,)),
                dma((ENC,)),
                dma((ENC, 4)),
                dma((2, ENC, 4)),
                dma((ENC, FRAME, 2)),
                dma((ENC, FRAME, 2)),
            ],
            compiler_params=pltpu.CompilerParams(
                collective_id=0, has_side_effects=True, vmem_limit_bytes=60 << 20
            ),
            name="sense_tv",
        )(
            kspace.reshape(2, NR, ENC, NC, NCOL),
            coil_maps.reshape(2, NR, NC, NCOL),
            sampling_masks.reshape(ENC, 1, NR),
            start_image.reshape(ROWS, 2 * ENC, 1, NCOL),
            jnp.asarray(forward_table),
            jnp.asarray(adjoint_table),
        )
        image, dual = pl.pallas_call(
            restore,
            out_shape=(
                jax.ShapeDtypeStruct((ROWS, 2 * ENC, 1, NCOL), F32),
                jax.ShapeDtypeStruct((4, ROWS, 2 * ENC, 1, NCOL), F32),
            ),
            in_specs=[hbm, hbm],
            out_specs=(hbm, hbm),
            scratch_shapes=[
                pltpu.VMEM((ENC, FRAME, 5, 2, PART, NCOL), I16),
                pltpu.VMEM((ENC, FRAME, 1, NCOL), F32),
                pltpu.VMEM((ENC, 5, 2, ROWS, NCOL), F32),
                dma((ENC + 1,)),
                dma((ENC, 5, 2)),
            ],
            compiler_params=pltpu.CompilerParams(vmem_limit_bytes=60 << 20),
            name="restore",
        )(coded, unit)
        return (
            image.reshape(ROWS, 2, ENC, 1, 1, NCOL),
            dual.reshape(4, ROWS, 2, ENC, 1, 1, NCOL),
        )

    return jax.shard_map(
        shards,
        mesh=mesh,
        in_specs=(
            P(None, None, None, "frame", "cuts", "coil", None),
            P(None, None, "cuts", "coil", None),
            P("frame", None, None),
            P("coil", None, None, "frame", "cuts", None),
        ),
        out_specs=(
            P("coil", None, None, "frame", "cuts", None),
            P(None, "coil", None, None, "frame", "cuts", None),
        ),
        check_vma=False,
    )
```

```python
import functools

import jax
import jax.numpy as jnp
import ml_dtypes
import numpy as np
from jax import lax
from jax.experimental import pallas as pl
from jax.experimental.pallas import tpu as pltpu
from jax.sharding import PartitionSpec as P

OUTER = 2
TV_ITERS = 3
STAGES = TV_ITERS + 4

DATA_STEP = 0.5
DUAL_STEP = 0.25
PRIMAL_STEP = 0.25
SMOOTH_WEIGHT = 0.3

MESH = pl.DeviceIdType.MESH
BF16 = jnp.bfloat16
F32 = jnp.float32
I16 = jnp.int16
CODES = 32000.0


def transform_tables(length):
    position = np.arange(length, dtype=np.int64)
    phase_grid = (position[:, None] * position[None, :]) % length
    angles = phase_grid.astype(np.float32) * np.float32(2.0 * np.pi / length)
    norming = np.float32(1.0) / np.sqrt(np.float32(length))
    real_part = (np.cos(angles) * norming).astype(ml_dtypes.bfloat16)
    imag_part = (-np.sin(angles) * norming).astype(ml_dtypes.bfloat16)
    forward_table = np.block([[real_part, -imag_part], [imag_part, real_part]])
    adjoint_table = np.block([[real_part, imag_part], [-imag_part, real_part]])
    return forward_table, adjoint_table


def coded_as(values, per_unit):
    return jnp.round(values * per_unit).astype(jnp.int32).astype(I16)


def project(real_part, imag_part):
    factor = jnp.minimum(
        SMOOTH_WEIGHT * lax.rsqrt(real_part * real_part + imag_part * imag_part), 1.0
    )
    return real_part * factor, imag_part * factor


def kernel(
    sizes,
    kspace_hbm, maps_hbm, mask_hbm, image_hbm, forward_hbm, adjoint_hbm,
    coded_out, unit_out,
    kspace_raw, maps_raw, kspace_ref, maps_ref, forward_ref, adjoint_ref, masked_ref,
    mask_ref, image_ref, rounded, gathered, coil_data, residual, partial, coded, unit, arrived, units,
    primal, anchor, bar, dual, rim_rows, rim_slices, edges, halo_rows, halo_wide,
    last, last_unit,
    load_sem, first_send, first_recv, start_send, start_recv, ag_send, ag_recv,
    rs_send, rs_recv, unit_send, unit_recv, halo_send, halo_recv, out_send, out_recv,
):
    NR, NCOL, NC, ENC, COIL, CUTS, FRAME = sizes
    ROWS = NR // COIL
    PART = ROWS // FRAME
    LOW = COIL // 4
    WIDE = LOW * FRAME
    BLOCKS = 4 * WIDE
    me = lax.axis_index("coil")
    cut = lax.axis_index("cuts")
    frame = lax.axis_index("frame")
    my_y, my_x = lax.div(me, LOW), frame * LOW + lax.rem(me, LOW)

    def place(y, x):
        return {"coil": y * LOW + lax.rem(x, LOW), "frame": lax.div(x, LOW)}

    def turned(y, x):
        return jnp.where(lax.rem(y, 2) == 0, x, WIDE - 1 - x)

    def block_of(y, x):
        return y * WIDE + turned(y, x)

    def holder(block):
        y = lax.div(block, WIDE)
        return y, turned(y, lax.rem(block, WIDE))

    mine = block_of(my_y, my_x)
    my_block = pl.ds(pl.multiple_of(mine * PART, PART), PART)
    my_rows = pl.ds(pl.multiple_of(me * ROWS, ROWS), ROWS)
    my_place = frame * COIL + me

    offsets = [(dy, dx) for dy in range(4) for dx in range(WIDE) if (dy, dx) != (0, 0)]
    PEERS = len(offsets)
    there = [(lax.rem(my_y + dy, 4), lax.rem(my_x + dx, WIDE)) for dy, dx in offsets]
    places = [place(*t) for t in there]
    blocks = [block_of(*t) for t in there]
    frames = [lax.div(x, LOW) for _, x in there]
    above = place(*holder(lax.rem(mine + BLOCKS - 1, BLOCKS)))
    below = place(*holder(lax.rem(mine + 1, BLOCKS)))
    before, behind = {"cuts": lax.rem(cut + CUTS - 1, CUTS)}, {"cuts": lax.rem(cut + 1, CUTS)}

    barrier = pltpu.get_barrier_semaphore()
    greeted = places[::-1] + [before, behind]
    for other in greeted:
        pl.semaphore_signal(barrier, inc=1, device_id=other, device_id_type=MESH)

    def image_load(e, p):
        return pltpu.make_async_copy(
            image_hbm.at[:, p * ENC + e, 0, :], image_ref.at[e, p], load_sem.at[2 * e + p]
        )

    def plain_load(src, dst, i):
        return pltpu.make_async_copy(src, dst, load_sem.at[2 * ENC + i])

    loads = [
        plain_load(maps_hbm, maps_raw, 0),
        plain_load(forward_hbm, forward_ref, 1),
        plain_load(kspace_hbm, kspace_raw, 2),
        plain_load(adjoint_hbm, adjoint_ref, 3),
        plain_load(mask_hbm, mask_ref, 4),
    ]
    for e in range(ENC):
        for p in range(2):
            image_load(e, p).start()
    for load in loads:
        load.start()

    for e in range(ENC):
        for p in range(2):
            image_load(e, p).wait()
            gathered[e, p, my_rows, :] = image_ref[e, p].astype(BF16)
    pl.semaphore_wait(barrier, len(greeted))

    def first_copy(e, d):
        other = {"coil": lax.rem(me + 1 + d, COIL)}
        return pltpu.make_async_remote_copy(
            gathered.at[e, :, my_rows, :], gathered.at[e, :, my_rows, :],
            first_send.at[e], first_recv.at[e], device_id=other, device_id_type=MESH,
        )

    def all_of(part, send, recv):
        return pltpu.make_async_remote_copy(
            part, part, send, recv, device_id=before, device_id_type=MESH
        )

    def first_all(e):
        rows = pl.ds(0, (COIL - 1) * ROWS)
        return all_of(gathered.at[e, :, rows, :], first_send.at[e], first_recv.at[e])

    def ag_all(e):
        rows = pl.ds(0, PEERS * PART)
        return all_of(gathered.at[e, :, rows, :], ag_send.at[e], ag_recv.at[e])

    def rs_all(e):
        return all_of(arrived.at[e, pl.ds(0, PEERS)], rs_send.at[e], rs_recv.at[e])

    def unit_all(e):
        return all_of(units.at[e, pl.ds(0, PEERS)], unit_send.at[e], unit_recv.at[e])

    def start_block(k):
        return my_y * WIDE + lax.rem(me, LOW) * FRAME + k

    def start_remote(k):
        return pltpu.make_async_remote_copy(
            image_ref.at[:, :, pl.ds(k * PART, PART), :], primal.at[frame],
            start_send.at[k], start_recv.at[frame],
            device_id=place(*holder(start_block(k))), device_id_type=MESH,
        )

    def start_local(k):
        return pltpu.make_async_copy(
            image_ref.at[:, :, pl.ds(k * PART, PART), :], primal.at[frame], start_send.at[k]
        )

    def ag_copy(e, d):
        return pltpu.make_async_remote_copy(
            rounded.at[e, frames[d]], gathered.at[e, :, my_block, :],
            ag_send.at[e], ag_recv.at[e],
            device_id=places[d], device_id_type=MESH,
        )

    def rs_copy(e, d):
        return pltpu.make_async_remote_copy(
            coded.at[e, blocks[d]], arrived.at[e, my_place],
            rs_send.at[e], rs_recv.at[e],
            device_id=places[d], device_id_type=MESH,
        )

    def unit_copy(e, d):
        return pltpu.make_async_remote_copy(
            unit.at[e], units.at[e, my_place], unit_send.at[e], unit_recv.at[e],
            device_id=places[d], device_id_type=MESH,
        )

    def halo_copies(e, parity):
        plan = [
            (edges.at[e, 0], halo_rows.at[parity, e, 0], below),
            (edges.at[e, 1], halo_rows.at[parity, e, 1], above),
            (bar.at[e], halo_wide.at[parity, e, 0], behind),
            (bar.at[e], halo_wide.at[parity, e, 1], before),
        ]
        return [
            pltpu.make_async_remote_copy(
                src, dst, halo_send.at[e, i // 2], halo_recv.at[parity, e, i // 2],
                device_id=to, device_id_type=MESH,
            )
            for i, (src, dst, to) in enumerate(plan)
        ]

    def halo_all(e, parity):
        return [
            all_of(part, halo_send.at[e, i], halo_recv.at[parity, e, i])
            for i, part in enumerate([halo_rows.at[parity, e], halo_wide.at[parity, e]])
        ]

    my_turn = turned(my_y, my_x)
    my_half = lax.rem(my_turn, FRAME)

    def owner(f):
        return my_y, f * LOW + lax.div(my_turn, FRAME)

    def out_remote(e, f):
        to = place(*owner(f))
        return [
            pltpu.make_async_remote_copy(
                src, dst, out_send.at[e, f, i], out_recv.at[e, my_half, i],
                device_id=to, device_id_type=MESH,
            )
            for i, (src, dst) in enumerate(
                [(last.at[e, f], coded_out.at[e, my_half]), (last_unit.at[e], unit_out.at[e, my_half])]
            )
        ]

    def out_local(e, f):
        return [
            pltpu.make_async_copy(last.at[e, f], coded_out.at[e, my_half], out_send.at[e, f, 0]),
            pltpu.make_async_copy(last_unit.at[e], unit_out.at[e, my_half], out_send.at[e, f, 1]),
        ]

    def out_arrival(e, half):
        return [
            pltpu.make_async_remote_copy(
                dst, dst, out_send.at[e, 0, i], out_recv.at[e, half, i],
                device_id=before, device_id_type=MESH,
            )
            for i, dst in enumerate([coded_out.at[e, half], unit_out.at[e, half]])
        ]

    for e in range(ENC):
        for d in range(COIL - 1):
            first_copy(e, d).start()
    for k in range(FRAME):
        y, x = holder(start_block(k))

        @pl.when(x != my_x)
        def _():
            start_remote(k).start()

        @pl.when(x == my_x)
        def _():
            start_local(k).start()

    row_id = lax.broadcasted_iota(jnp.int32, (256, 256), 0)
    col_id = lax.broadcasted_iota(jnp.int32, (256, 256), 1)
    source = jnp.where(row_id < 128, 2 * row_id, 2 * row_id - 255)
    sort_rows = jnp.where(col_id == source, 1.0, 0.0).astype(BF16)

    def sorted_pair(block):
        return jnp.dot(
            sort_rows, block.reshape(256, NCOL), preferred_element_type=F32
        ).astype(BF16)

    loads[0].wait()
    for p in range(2):
        def maps_part(i, carry):
            rows = pl.ds(pl.multiple_of(i * 128, 128), 128)
            both = sorted_pair(maps_raw[p, rows])
            maps_ref[p, 0, rows, :] = both[:128]
            maps_ref[p, 1, rows, :] = both[128:]
            return carry

        lax.fori_loop(0, NR // 128, maps_part, 0)
    loads[2].wait()
    for p in range(2):
        def kspace_part(i, carry):
            e, part = lax.rem(i, ENC), lax.div(i, ENC)
            rows = pl.ds(pl.multiple_of(part * 128, 128), 128)
            both = sorted_pair(kspace_raw[p, rows, e])
            kspace_ref[e, p, 0, rows, :] = both[:128]
            kspace_ref[e, p, 1, rows, :] = both[128:]
            return carry

        lax.fori_loop(0, ENC * NR // 128, kspace_part, 0)
    loads[3].wait()
    loads[4].wait()

    def mask_part(i, carry):
        e, part = lax.rem(i, ENC), lax.div(i, ENC)
        rows = pl.ds(pl.multiple_of(part * 64, 64), 64)
        sampled = mask_ref[e].astype(F32)
        for p in range(2):
            columns = pl.ds(p * NR, NR)
            masked_ref[e, rows, columns] = (
                adjoint_ref[rows, columns].astype(F32) * sampled
            ).astype(BF16)
        return carry

    lax.fori_loop(0, ENC * 2 * NR // 64, mask_part, 0)
    dual[...] = jnp.zeros_like(dual)
    rim_rows[...] = jnp.zeros_like(rim_rows)
    rim_slices[...] = jnp.zeros_like(rim_slices)
    edges[...] = jnp.zeros_like(edges)
    loads[1].wait()
    def data_stage(e, outer):
        @pl.when(outer == 0)
        def _():
            first_all(e).wait_recv()

        @pl.when(outer != 0)
        def _():
            ag_all(e).wait_recv()

        for c in range(NC):
            map_real, map_imag = maps_ref[0, c].astype(F32), maps_ref[1, c].astype(F32)
            image_real, image_imag = gathered[e, 0].astype(F32), gathered[e, 1].astype(F32)
            coil_data[c, :NR] = (map_real * image_real - map_imag * image_imag).astype(BF16)
            coil_data[c, NR:] = (map_real * image_imag + map_imag * image_real).astype(BF16)
            for p in range(2):
                spectrum = jnp.dot(
                    forward_ref[p * NR : (p + 1) * NR], coil_data[c], preferred_element_type=F32
                )
                residual[c, p * NR : (p + 1) * NR] = (
                    spectrum - kspace_ref[e, p, c].astype(F32)
                ).astype(BF16)
        for c in range(NC):
            map_real, map_imag = maps_ref[0, c].astype(F32), maps_ref[1, c].astype(F32)
            back_real = jnp.dot(masked_ref[e, :NR], residual[c], preferred_element_type=F32)
            back_imag = jnp.dot(masked_ref[e, NR:], residual[c], preferred_element_type=F32)
            grad_real = (map_real * back_real + map_imag * back_imag).reshape(BLOCKS, PART, NCOL)
            grad_imag = (map_real * back_imag - map_imag * back_real).reshape(BLOCKS, PART, NCOL)
            if c == 0:
                partial[:, 0], partial[:, 1] = grad_real, grad_imag
            else:
                partial[:, 0] += grad_real
                partial[:, 1] += grad_imag
        top = jnp.max(jnp.abs(partial[...]), axis=(0, 1, 2), keepdims=True)[0, 0]
        step = jnp.maximum(top, 1e-30) * (1.0 / CODES)
        unit[e] = step
        coded[e] = coded_as(partial[...], 1.0 / step)
        for d in range(PEERS):
            unit_copy(e, d).start()
            rs_copy(e, d).start()
        units[e, my_place] = step
        arrived[e, my_place] = coded[e, mine]

        @pl.when(outer == 0)
        def _():
            first_all(e).wait_send()

        @pl.when(outer != 0)
        def _():
            ag_all(e).wait_send()

    def publish(e, x, parity):
        for f in range(FRAME):
            for p in range(2):
                bar[e, f, p] = x[f][p]
                i = 2 * f + p
                edges[e, 0, i : i + 1, :] = x[f][p][PART - 1 : PART]
                edges[e, 1, i : i + 1, :] = x[f][p][0:1]
        for copy in halo_copies(e, parity):
            copy.start()

    def start_wait():
        for k in range(FRAME):
            y, x = holder(start_block(k))

            @pl.when(x != my_x)
            def _():
                start_remote(k).wait_send()

            @pl.when(x == my_x)
            def _():
                start_local(k).wait()

        for f in range(FRAME):
            @pl.when(owner(f)[1] != my_x)
            def _():
                pltpu.make_async_remote_copy(
                    primal.at[f], primal.at[f], start_send.at[0], start_recv.at[f],
                    device_id=before, device_id_type=MESH,
                ).wait_recv()

    def anchor_stage(e, outer):
        pl.when(jnp.logical_and(e == 0, outer == 0))(start_wait)
        unit_all(e).wait_recv()
        rs_all(e).wait_recv()
        x = [[None, None], [None, None]]
        for f in range(FRAME):
            for p in range(2):
                total = jnp.zeros((PART, NCOL), F32)
                for c in range(f * COIL, f * COIL + COIL):
                    total = total + arrived[e, c, p].astype(F32) * units[e, c]
                x[f][p] = primal[f, e, p] - DATA_STEP * total
                anchor[e, f, p] = x[f][p]
                primal[f, e, p] = x[f][p]
        publish(e, x, lax.rem(outer * TV_ITERS, 2))
        unit_all(e).wait_send()
        rs_all(e).wait_send()

    rows_at = lax.broadcasted_iota(jnp.int32, (PART, NCOL), 0)
    cols_at = lax.broadcasted_iota(jnp.int32, (PART, NCOL), 1)
    last_row = rows_at == PART - 1
    first_row = rows_at == 0
    row_keep = jnp.where(jnp.logical_and(last_row, mine == BLOCKS - 1), 0.0, DUAL_STEP)
    rim_keep = jnp.where(mine == 0, 0.0, 1.0)
    slice_keep = jnp.where(cut == CUTS - 1, 0.0, DUAL_STEP)
    rim_slice_keep = jnp.where(cut == 0, 0.0, 1.0)
    col_keep = jnp.where(cols_at == NCOL - 1, 0.0, DUAL_STEP)
    col_back = jnp.where(cols_at == 0, 0.0, 1.0)

    def tv_stage(e, it, outer):
        parity = lax.rem(outer * TV_ITERS + it, 2)
        for copy in halo_all(e, parity):
            copy.wait_recv()
            copy.wait_send()
        both = [[bar[e, f, p] for p in range(2)] for f in range(FRAME)]
        swing = project(*[
            dual[e, 3, 0, p] + DUAL_STEP * (both[1][p] - both[0][p]) for p in range(2)
        ])
        fresh = [[None, None], [None, None]]
        for p in range(2):
            dual[e, 3, 0, p] = swing[p]
            dual[e, 3, 1, p] = -swing[p]
        for f in range(FRAME):
            x = both[f]

            def stepped(k, diffs):
                new = project(*[dual[e, k, f, p] + diffs[p] for p in range(2)])
                for p in range(2):
                    dual[e, k, f, p] = new[p]
                return new

            after = [halo_rows[parity, e, 1, 2 * f + p : 2 * f + p + 1, :] for p in range(2)]
            prior = [halo_rows[parity, e, 0, 2 * f + p : 2 * f + p + 1, :] for p in range(2)]
            rows = stepped(0, [
                row_keep * (jnp.where(last_row, after[p], pltpu.roll(x[p], PART - 1, 0)) - x[p])
                for p in range(2)
            ])
            rim = project(*[
                rim_rows[e, f, p] + DUAL_STEP * (x[p][0:8] - prior[p]) for p in range(2)
            ])
            spread = [None, None]
            for p in range(2):
                edge = rim[p] * rim_keep
                rim_rows[e, f, p] = edge
                spread[p] = rows[p] - jnp.where(first_row, edge[0:1], pltpu.roll(rows[p], 1, 0))
            cols = stepped(1, [col_keep * (pltpu.roll(x[p], NCOL - 1, 1) - x[p]) for p in range(2)])
            for p in range(2):
                spread[p] = spread[p] + (cols[p] - col_back * pltpu.roll(cols[p], 1, 1))
            cuts = stepped(2, [slice_keep * (halo_wide[parity, e, 1, f, p] - x[p]) for p in range(2)])
            rim = project(*[
                rim_slices[e, f, p] + DUAL_STEP * (x[p] - halo_wide[parity, e, 0, f, p])
                for p in range(2)
            ])
            for p in range(2):
                edge = rim[p] * rim_slice_keep
                rim_slices[e, f, p] = edge
                spread[p] = spread[p] + (cuts[p] - edge)
            for p in range(2):
                spread[p] = spread[p] + (2.0 - 4.0 * f) * swing[p]
                held = primal[f, e, p]
                updated = (held + PRIMAL_STEP * spread[p] + PRIMAL_STEP * anchor[e, f, p]) * (
                    1.0 / (1.0 + PRIMAL_STEP)
                )
                primal[f, e, p] = updated
                fresh[f][p] = 2.0 * updated - held

        @pl.when(it < TV_ITERS - 1)
        def _():
            publish(e, fresh, 1 - parity)

        @pl.when(jnp.logical_and(it == TV_ITERS - 1, outer < OUTER - 1))
        def _():
            for f in range(FRAME):
                for p in range(2):
                    rounded[e, f, p] = primal[f, e, p].astype(BF16)
            for d in range(PEERS):
                ag_copy(e, d).start()
            for p in range(2):
                gathered[e, p, my_block, :] = rounded[e, frame, p]

        @pl.when(jnp.logical_and(it == TV_ITERS - 1, outer == OUTER - 1))
        def _():
            top = jnp.max(jnp.abs(primal[:, e]), axis=(0, 1, 2), keepdims=True)[0, 0]
            step = jnp.maximum(top, 1e-30) * (1.0 / CODES)
            last_unit[e] = step
            for f in range(FRAME):
                last[e, f, 4] = coded_as(primal[f, e], 1.0 / step)
                for k in range(4):
                    last[e, f, k] = coded_as(dual[e, k, f], CODES / SMOOTH_WEIGHT)
            for f in range(FRAME):
                @pl.when(owner(f)[1] != my_x)
                def _():
                    for copy in out_remote(e, f):
                        copy.start()

                @pl.when(owner(f)[1] == my_x)
                def _():
                    for copy in out_local(e, f):
                        copy.start()

    def slot(t, carry):
        def one(i, carry):
            e = ENC - 1 - i
            at = t - e
            outer = lax.div(at, STAGES)
            stage = lax.rem(at, STAGES)
            active = jnp.logical_and(at >= 0, at < OUTER * STAGES)

            @pl.when(jnp.logical_and(active, stage == 0))
            def _():
                data_stage(e, outer)

            @pl.when(jnp.logical_and(active, stage == 2))
            def _():
                anchor_stage(e, outer)

            @pl.when(jnp.logical_and(active, jnp.logical_and(stage >= 3, stage < 3 + TV_ITERS)))
            def _():
                tv_stage(e, stage - 3, outer)

            return carry

        return lax.fori_loop(0, ENC, one, carry)

    lax.fori_loop(0, OUTER * STAGES + ENC - 1, slot, 0)

    def finish(e, carry):
        for f in range(FRAME):
            @pl.when(owner(f)[1] != my_x)
            def _():
                for copy in out_remote(e, f):
                    copy.wait_send()

            @pl.when(owner(f)[1] == my_x)
            def _():
                for copy in out_local(e, f):
                    copy.wait()

        for half in range(FRAME):
            @pl.when(holder(start_block(half))[1] != my_x)
            def _():
                for copy in out_arrival(e, half):
                    copy.wait_recv()

        return carry

    lax.fori_loop(0, ENC, finish, 0)


def restore(coded_hbm, unit_hbm, image_out, dual_out, coded, unit, values, load_sem, out_sem):
    ENC, FRAME, KINDS, _, PART, NCOL = coded.shape
    loads = [pltpu.make_async_copy(unit_hbm, unit, load_sem.at[ENC])]
    loads += [
        pltpu.make_async_copy(coded_hbm.at[e], coded.at[e], load_sem.at[e]) for e in range(ENC)
    ]
    for load in loads:
        load.start()
    loads[0].wait()

    def stores(e):
        copies = []
        for p in range(2):
            for k in range(KINDS):
                if k == KINDS - 1:
                    to = image_out.at[:, p * ENC + e, 0, :]
                else:
                    to = dual_out.at[k, :, p * ENC + e, 0, :]
                copies.append(
                    pltpu.make_async_copy(values.at[e, k, p], to, out_sem.at[e, k, p])
                )
        return copies

    for e in range(ENC):
        loads[1 + e].wait()
        for half in range(FRAME):
            rows = pl.ds(half * PART, PART)
            for p in range(2):
                for k in range(KINDS):
                    step = unit[e, half] if k == KINDS - 1 else SMOOTH_WEIGHT / CODES
                    values[e, k, p, rows, :] = coded[e, half, k, p].astype(F32) * step
        for copy in stores(e):
            copy.start()
    for e in range(ENC):
        for copy in stores(e):
            copy.wait()


def solution(mesh):
    COIL, CUTS, FRAME = mesh.shape["coil"], mesh.shape["cuts"], mesh.shape["frame"]

    def shards(kspace, coil_maps, sampling_masks, start_image):
        _, NR, ENC, _, _, NC, NCOL = kspace.shape
        ROWS = start_image.shape[0]
        PART = ROWS // FRAME
        forward_table, adjoint_table = transform_tables(NR)
        hbm = pl.BlockSpec(memory_space=pltpu.HBM)
        dma = pltpu.SemaphoreType.DMA
        coded, unit = pl.pallas_call(
            functools.partial(kernel, (NR, NCOL, NC, ENC, COIL, CUTS, FRAME)),
            out_shape=(
                jax.ShapeDtypeStruct((ENC, FRAME, 5, 2, PART, NCOL), I16),
                jax.ShapeDtypeStruct((ENC, FRAME, 1, NCOL), F32),
            ),
            in_specs=[hbm] * 6,
            out_specs=(hbm, hbm),
            scratch_shapes=[
                pltpu.VMEM((2, NR, ENC, NC, NCOL), BF16),
                pltpu.VMEM((2, NR, NC, NCOL), BF16),
                pltpu.VMEM((ENC, 2, NC, NR, NCOL), BF16),
                pltpu.VMEM((2, NC, NR, NCOL), BF16),
                pltpu.VMEM((2 * NR, 2 * NR), BF16),
                pltpu.VMEM((2 * NR, 2 * NR), BF16),
                pltpu.VMEM((ENC, 2 * NR, 2 * NR), BF16),
                pltpu.VMEM((ENC, 1, NR), jnp.int32),
                pltpu.VMEM((ENC, 2, ROWS, NCOL), F32),
                pltpu.VMEM((ENC, FRAME, 2, PART, NCOL), BF16),
                pltpu.VMEM((ENC, 2, NR, NCOL), BF16),
                pltpu.VMEM((NC, 2 * NR, NCOL), BF16),
                pltpu.VMEM((NC, 2 * NR, NCOL), BF16),
                pltpu.VMEM((NR // PART, 2, PART, NCOL), F32),
                pltpu.VMEM((ENC, NR // PART, 2, PART, NCOL), I16),
                pltpu.VMEM((ENC, 1, NCOL), F32),
                pltpu.VMEM((ENC, FRAME * COIL, 2, PART, NCOL), I16),
                pltpu.VMEM((ENC, FRAME * COIL, 1, NCOL), F32),
                pltpu.VMEM((FRAME, ENC, 2, PART, NCOL), F32),
                pltpu.VMEM((ENC, FRAME, 2, PART, NCOL), F32),
                pltpu.VMEM((ENC, FRAME, 2, PART, NCOL), F32),
                pltpu.VMEM((ENC, 4, FRAME, 2, PART, NCOL), F32),
                pltpu.VMEM((ENC, FRAME, 2, 8, NCOL), F32),
                pltpu.VMEM((ENC, FRAME, 2, PART, NCOL), F32),
                pltpu.VMEM((ENC, 2, 8, NCOL), F32),
                pltpu.VMEM((2, ENC, 2, 8, NCOL), F32),
                pltpu.VMEM((2, ENC, 2, FRAME, 2, PART, NCOL), F32),
                pltpu.VMEM((ENC, FRAME, 5, 2, PART, NCOL), I16),
                pltpu.VMEM((ENC, 1, NCOL), F32),
                dma((2 * ENC + 5,)),
                dma((ENC,)),
                dma((ENC,)),
                dma((FRAME,)),
                dma((FRAME,)),
                dma((ENC,)),
                dma((ENC,)),
                dma((ENC,)),
                dma((ENC,)),
                dma((ENC,)),
                dma((ENC,)),
                dma((ENC, 2)),
                dma((2, ENC, 2)),
                dma((ENC, FRAME, 2)),
                dma((ENC, FRAME, 2)),
            ],
            compiler_params=pltpu.CompilerParams(
                collective_id=0, has_side_effects=True, vmem_limit_bytes=60 << 20
            ),
            name="sense_tv",
        )(
            kspace.reshape(2, NR, ENC, NC, NCOL),
            coil_maps.reshape(2, NR, NC, NCOL),
            sampling_masks.reshape(ENC, 1, NR),
            start_image.reshape(ROWS, 2 * ENC, 1, NCOL),
            jnp.asarray(forward_table),
            jnp.asarray(adjoint_table),
        )
        image, dual = pl.pallas_call(
            restore,
            out_shape=(
                jax.ShapeDtypeStruct((ROWS, 2 * ENC, 1, NCOL), F32),
                jax.ShapeDtypeStruct((4, ROWS, 2 * ENC, 1, NCOL), F32),
            ),
            in_specs=[hbm, hbm],
            out_specs=(hbm, hbm),
            scratch_shapes=[
                pltpu.VMEM((ENC, FRAME, 5, 2, PART, NCOL), I16),
                pltpu.VMEM((ENC, FRAME, 1, NCOL), F32),
                pltpu.VMEM((ENC, 5, 2, ROWS, NCOL), F32),
                dma((ENC + 1,)),
                dma((ENC, 5, 2)),
            ],
            compiler_params=pltpu.CompilerParams(vmem_limit_bytes=60 << 20),
            name="restore",
        )(coded, unit)
        return (
            image.reshape(ROWS, 2, ENC, 1, 1, NCOL),
            dual.reshape(4, ROWS, 2, ENC, 1, 1, NCOL),
        )

    return jax.shard_map(
        shards,
        mesh=mesh,
        in_specs=(
            P(None, None, None, "frame", "cuts", "coil", None),
            P(None, None, "cuts", "coil", None),
            P("frame", None, None),
            P("coil", None, None, "frame", "cuts", None),
        ),
        out_specs=(
            P("coil", None, None, "frame", "cuts", None),
            P(None, "coil", None, None, "frame", "cuts", None),
        ),
        check_vma=False,
    )
```
